32 devices in a mesh: groups: 2 (over y), adapter: 8 (over z, x), fsdp: 2 (over core).
Axes of the slice: x: 2, y: 2, z: 4, core: 2. Of those that a mesh axis runs over, the one named last changes fastest.
Arguments:
- hidden: bfloat16 [3840, 8192], P(('groups', 'adapter', 'fsdp')), parts along dimension 0, may hold values from -6 to 6
- adapter_ids: int32 [3840, 1], P(('groups', 'adapter', 'fsdp')), parts along dimension 0, may hold values from 0 to 7; in each aligned block of 120 rows (0 to 119, 120 to 239, ...) at most 30 rows name the same one
- owner_map: int32 [8], replicated, may hold values from 0 to 7, each once
- down_a: bfloat16 [8, 8192, 64], P('adapter', 'fsdp'), may hold values from -0.0625 to 0.0625
- up_b: bfloat16 [8, 64, 8192], P('adapter', None, 'fsdp'), may hold values from -0.75 to 0.75
- norm_gain: bfloat16 [8192], P('fsdp'), may hold values from 0.5 to 1.5
- reward_head: bfloat16 [8192], P('fsdp'), may hold values from -0.0625 to 0.0625
Outputs:
- adapted: bfloat16 [3840, 8192], P(('groups', 'adapter', 'fsdp')), parts along dimension 0
- scores: float32 [3840], P(('groups', 'adapter', 'fsdp')), parts along dimension 0
The draws below stay inside these ranges and needn't reach their ends.
There are 2 independent parts, one for each index of `groups`. The reference program is written for one: setup_inputs(seed, part) draws one part's arguments, and reference() takes and returns one part's arrays. A program takes and returns all parts, laid end to end along the dimension named above; an argument that names none is the same for every part. Nothing has to cross between parts.
Inputs may be any that keep to these rules, and one draw needn't show every extreme that they name: `adapter_ids`: the rows of one device name any one adapter at most 30 times; some adapter exactly 30 times. `owner_map`: each position appears once.
All inputs are finite; a program needn't handle non-finite values.
Results may differ from the reference program's by a relative error of at most 0.007.
Values may be sent and summed in bfloat16 or wider, within the bound.
No kernel may reach another device: no remote copies, remote signals or barrier semaphores. Data moves between devices by JAX's collectives and lax.ppermute only.
A program may use at most 64 MiB of HBM per device.

```python
import math
import jax
import jax.numpy as jnp
import numpy as np
from jax import lax

D = 8192
R = 64
TOK_DEV = 120
ADAPTERS = 8
CAP = 30
TOKENS = 1920
N_ADAPTER = 8
N_FSDP = 2


def block_levels(own_key, dims, split, low, top_value):
    factor_of = 1.0
    for dim, parts in split:
        steps = jax.random.uniform(jax.random.fold_in(jax.random.fold_in(own_key, 6), dim), (parts,), jnp.float32, low / len(split), top_value / len(split))
        factor_of = factor_of * jnp.repeat(jnp.exp(steps), dims[dim] // parts).reshape((-1,) + (1,) * (len(dims) - 1 - dim))
    return factor_of


def routed_block(rng, own, number, rows, amount, top, most, lean):
    ranking = jax.random.permutation(rng, amount)
    heavy_load, usual = load_shares(amount, rows * top, most, lean, True), load_shares(amount, rows * top, most, lean, False)
    places = jnp.arange(amount)

    def named(tallies, turn):
        used = int((tallies > 0).sum())
        fixed = max(1, used // 4)
        moved = fixed + (places - fixed + turn * (used - fixed)) % max(1, amount - fixed)
        return jnp.zeros((amount,), jnp.int32).at[ranking[jnp.where(places < fixed, places, moved)]].set(jnp.asarray(tallies, jnp.int32))

    tallies = jnp.where(number % 4 == 0, named(heavy_load, number // 4), named(usual, number - number // 4 - 1))
    mixed = jax.random.permutation(jax.random.fold_in(own, 3), amount)
    giver, sink = mixed[0:amount // 2 * 2:2], mixed[1:amount // 2 * 2:2]
    room = jnp.minimum(tallies[giver] - 1, most - tallies[sink]) // 2
    room = jnp.where((giver == ranking[0]) | (sink == ranking[0]) | (tallies[sink] == 0), 0, jnp.maximum(room, 0))
    moved = jax.random.randint(jax.random.fold_in(own, 4), (amount // 2,), 0, 1 << 20) % (room + 1)
    tallies = tallies.at[giver].add(-moved).at[sink].add(moved)
    items = jnp.searchsorted(jnp.cumsum(tallies), jnp.arange(rows * top), side="right").astype(jnp.int32)
    grid = items.reshape(top, rows).T
    grid = grid[jax.random.permutation(jax.random.fold_in(own, 1), rows)]
    turn = jax.random.randint(jax.random.fold_in(own, 2), (rows, 1), 0, top)
    return jnp.take_along_axis(grid, (jnp.arange(top)[None, :] + turn) % top, axis=1)


def load_shares(number_of, total, bound, skew, full):
    weights = [(1 << 20) // math.isqrt(grade ** skew) + 1 for grade in range(1, number_of + 1)]
    largest = bound if full else min(bound, max(-(-total // number_of), total * weights[0] // sum(weights)))
    least = 1 if total - largest >= number_of - 1 else 0
    given, spare = [largest] + [least] * (number_of - 1), total - largest - least * (number_of - 1)
    while spare > 0:
        free = [i for i in range(1, number_of) if given[i] < largest] or [i for i in range(1, number_of) if given[i] < bound]
        whole, budget = sum([weights[i] for i in free]), spare
        for i in free:
            addition = min(bound - given[i], max(1, budget * weights[i] // whole), spare)
            given[i] = given[i] + addition
            spare = spare - addition
    return np.array(given)


def normal_values(stream_key, extent, scale, limit, pieces=(), held_as=jnp.bfloat16):
    loudness = block_levels(stream_key, extent, pieces, -0.22, 0.18) if pieces else 1.0
    result = jax.random.normal(stream_key, extent, jnp.float32) * scale * loudness
    return jnp.minimum(jnp.maximum(result, -limit), limit).astype(held_as)


def setup_inputs(seed: int = 0, part: int = 0) -> dict:
    seeds = jax.random.split(jax.random.key(seed), 8)
    part_keys = jax.random.split(jax.random.fold_in(seeds[7], part), 8)
    hidden = normal_values(part_keys[0], (TOKENS, D), 1.0, 6.0, ((0, 16),))
    adapter_ids_keys = jax.random.split(jax.random.fold_in(part_keys[1], 1), TOKENS // TOK_DEV)
    adapter_ids_turns = jax.random.permutation(jax.random.fold_in(part_keys[1], 3), TOKENS // TOK_DEV)
    adapter_ids = jax.vmap(lambda own, number: routed_block(jax.random.fold_in(part_keys[1], 2), own, number, TOK_DEV, ADAPTERS, 1, CAP, 2))(adapter_ids_keys, adapter_ids_turns).reshape((TOKENS, 1))
    owner_map = jax.random.permutation(seeds[2], ADAPTERS).astype(jnp.int32)
    down_a = normal_values(seeds[3], (ADAPTERS, D, R), D ** -0.5, 0.0625, ((0, 8), (1, 2)))
    up_b = normal_values(seeds[4], (ADAPTERS, R, D), R ** -0.5, 0.75, ((0, 8), (2, 2)))
    norm_gain = jnp.clip(1.0 + 0.1 * jax.random.normal(seeds[5], (D,), jnp.float32), 0.5, 1.5).astype(jnp.bfloat16)
    reward_head = normal_values(seeds[6], (D,), D ** -0.5, 0.0625, ((0, 2),))
    return {"hidden": hidden, "adapter_ids": adapter_ids, "owner_map": owner_map, "down_a": down_a, "up_b": up_b, "norm_gain": norm_gain, "reward_head": reward_head}


def reference(hidden, adapter_ids, owner_map, down_a, up_b, norm_gain, reward_head):
    values = hidden.astype(jnp.float32)
    factor = lax.rsqrt(lax.optimization_barrier(jnp.mean(values * values, axis=-1, keepdims=True)) + 1e-05)
    normed = (values * factor * norm_gain.astype(jnp.float32)).astype(jnp.bfloat16)
    slots = owner_map[adapter_ids[:, 0]].astype(jnp.int32)
    order = jnp.argsort(slots, stable=True).astype(jnp.int32)
    counts = lax.optimization_barrier(jnp.sum((slots[:, None] == jnp.arange(ADAPTERS, dtype=jnp.int32)[None, :]).astype(jnp.int32), axis=0))
    offsets = (jnp.cumsum(counts) - counts).astype(jnp.int32)
    span = CAP * N_ADAPTER * N_FSDP
    sorted_rows = jnp.concatenate([normed[order], jnp.zeros((span, D), jnp.bfloat16)], axis=0)
    initial = jnp.zeros((TOKENS + span, D), jnp.bfloat16)

    def step(carry, index):
        start = offsets[index]
        rows = lax.dynamic_slice_in_dim(sorted_rows, start, span, 0)
        live = (jnp.arange(span, dtype=jnp.int32) < counts[index])[:, None]
        codes = jnp.dot(rows, down_a[index], preferred_element_type=jnp.float32).astype(jnp.bfloat16)
        delta = jnp.dot(codes, up_b[index], preferred_element_type=jnp.float32).astype(jnp.bfloat16)
        current = lax.dynamic_slice_in_dim(carry, start, span, 0)
        updated = current + jnp.where(live, delta, jnp.zeros_like(delta))
        return (lax.dynamic_update_slice_in_dim(carry, updated, start, 0), None)
    carry, _ = lax.scan(step, initial, jnp.arange(ADAPTERS, dtype=jnp.int32))
    inverse = jnp.zeros((TOKENS,), jnp.int32).at[order].set(jnp.arange(TOKENS, dtype=jnp.int32))
    delta = carry[:TOKENS][inverse]
    adapted = (normed.astype(jnp.float32) + 2.0 * delta.astype(jnp.float32)).astype(jnp.bfloat16)
    scores = jnp.dot(adapted, reward_head, preferred_element_type=jnp.float32)
    return (adapted, scores)
```

```python
import jax
import jax.numpy as jnp
from jax import lax
from jax.experimental import pallas as pl
from jax.experimental.pallas import tpu as pltpu
from jax.sharding import PartitionSpec as P

GATHER_LIMIT = 12 << 20
VMEM_LIMIT = 40 << 20


def routed_rows(hidden, adapter_ids, owner_map, down_a, up_b, norm_gain, reward_head):
    gain, head = (
        lax.all_gather(norm_gain, "fsdp", axis=0, tiled=True),
        lax.all_gather(reward_head, "fsdp", axis=0, tiled=True),
    )
    values = hidden.astype(jnp.float32)
    factor = lax.rsqrt(jnp.mean(values * values, axis=-1, keepdims=True) + 1e-05)
    normed = (values * factor * gain.astype(jnp.float32)).astype(jnp.bfloat16)
    row_count, width = hidden.shape
    lanes = lax.axis_size("adapter")
    capacity = max(2, (2 * row_count + lanes - 1) // lanes)
    owners = owners_of(adapter_ids, owner_map)
    marks = (owners[:, None] == jnp.arange(lanes, dtype=jnp.int32)[None, :]).astype(jnp.int32)
    ranks = jnp.sum(jnp.cumsum(marks, axis=0) * marks, axis=1) - 1
    target = owners * capacity + ranks
    outgoing = jnp.zeros((lanes * capacity, width), jnp.bfloat16).at[target].set(normed)
    outgoing = outgoing.reshape(lanes, capacity, width)
    full_a, full_b = (
        lax.all_gather(down_a, "fsdp", axis=1, tiled=True),
        lax.all_gather(up_b, "fsdp", axis=2, tiled=True),
    )
    matrix_a = full_a[0]
    matrix_b = full_b[0]
    received = lax.all_to_all(outgoing, "adapter", split_axis=0, concat_axis=0, tiled=True)
    flat = received.reshape(-1, width)
    codes = jnp.dot(flat, matrix_a, preferred_element_type=jnp.float32).astype(jnp.bfloat16)
    delta = jnp.dot(codes, matrix_b, preferred_element_type=jnp.float32).astype(jnp.bfloat16)
    returned = lax.all_to_all(
        delta.reshape(received.shape), "adapter", split_axis=0, concat_axis=0, tiled=True
    )
    delta = returned.reshape(-1, width)[target]
    adapted = (normed.astype(jnp.float32) + 2.0 * delta.astype(jnp.float32)).astype(jnp.bfloat16)
    scores = jnp.dot(adapted, head, preferred_element_type=jnp.float32)
    return (adapted, scores)


def owners_of(adapter_ids, owner_map):
    table_size = owner_map.shape[0]
    picked = (
        adapter_ids[:, 0][:, None] == jnp.arange(table_size, dtype=jnp.int32)[None, :]
    ).astype(jnp.int32)
    return jnp.sum(picked * owner_map[None, :], axis=1)


def snake(count):
    return list(range(0, count, 2)) + list(range(1, count, 2))[::-1]


def ring_hops(count):
    hops = []
    for distance in range(1, count // 2 + 1):
        hops.append((distance, 1))
        if 2 * distance < count:
            hops.append((distance, -1))
    return hops


def ring_gather(own, order):
    count = len(order)
    perms = {
        way: [(order[i], order[(i + way) % count]) for i in range(count)] for way in (1, -1)
    }
    held = {1: own, -1: own}
    arrived = [own]
    for _, way in ring_hops(count):
        held[way] = lax.ppermute(held[way], "adapter", perms[way])
        arrived.append(held[way])
    return arrived


def norm_kernel(place, hidden, other, own_small, other_small, gain, own_out, other_out, send_out):
    y = place[1]
    half = other.shape[1]
    quarter = half // 2
    there = pl.multiple_of((1 - y) * quarter, quarter)
    g = gain[...].astype(jnp.float32)
    a = (hidden[...].astype(jnp.float32) * own_small[:, 0:1] * g).astype(jnp.bfloat16)
    own_out[...] = a
    b = (other[...].astype(jnp.float32) * other_small[:, 0:1] * g).astype(jnp.bfloat16)
    other_out[...] = b
    send_out[:, 0:quarter] = own_out[:, pl.ds(there, quarter)]
    send_out[:, quarter:half] = other_out[:, pl.ds(there, quarter)]
    lane = lax.broadcasted_iota(jnp.int32, (a.shape[0], 128), 1)
    marks = jnp.where(lane == 0, own_small[:, 1:2], other_small[:, 1:2])
    send_out[:, half:] = marks.astype(jnp.bfloat16)


def codes_kernel(place, own, other, across, own_small, other_small, ids, *rest):
    *downs, here_out, there_out = rest
    quarter = downs[0].shape[1]
    half = own.shape[1]
    start = pl.multiple_of(place[1] * quarter, quarter)
    wide = jnp.concatenate([d[...] for d in downs], axis=0)
    names = ids[...]

    def part(rows, slot):
        got = lax.dot_general(
            rows, wide, (((1,), (1,)), ((), ())), preferred_element_type=jnp.float32
        )
        got = jnp.where(slot == names, got, 0.0)
        total = got[:, 0:128]
        for i in range(128, got.shape[1], 128):
            total = total + got[:, i : i + 128]
        return total

    slots = across[:, half:].astype(jnp.float32)
    there_out[:, 0:128] = part(across[:, 0:quarter], slots[:, 0:1])
    there_out[:, 128:256] = part(across[:, quarter:half], slots[:, 1:2])
    here_out[:, 0:128] = part(own[:, pl.ds(start, quarter)], own_small[:, 1:2])
    here_out[:, 128:256] = part(other[:, pl.ds(start, quarter)], other_small[:, 1:2])


def delta_kernel(place, own, other, here, there, own_small, other_small, ids, head, *rest):
    *ups, own_out, other_out, scores_out, own_codes, other_codes = rest
    names = ids[...]

    @pl.when(pl.program_id(0) == 0)
    def _():
        scores_out[...] = jnp.zeros_like(scores_out)
        for total, small, out in (
            (here[:, 0:128] + there[:, 128:256], own_small, own_codes),
            (here[:, 128:256] + there[:, 0:128], other_small, other_codes),
        ):
            code = total + pltpu.roll(total, 64, 1)
            wide = jnp.concatenate([code] * (names.shape[1] // 128), axis=1)
            out[...] = jnp.where(small[:, 1:2] == names, wide, 0.0).astype(jnp.bfloat16)

    wide = jnp.concatenate([u[...] for u in ups], axis=0)
    weights = head[...].astype(jnp.float32)
    lane = lax.broadcasted_iota(jnp.int32, scores_out.shape, 1)
    for turn, (rows, codes, out) in enumerate(
        ((own, own_codes, own_out), (other, other_codes, other_out))
    ):
        delta = jnp.dot(codes[...], wide, preferred_element_type=jnp.float32)
        delta = delta.astype(jnp.bfloat16).astype(jnp.float32)
        adapted = (rows[...].astype(jnp.float32) + 2.0 * delta).astype(jnp.bfloat16)
        out[...] = adapted
        part = jnp.sum(adapted.astype(jnp.float32) * weights, axis=1, keepdims=True)
        scores_out[...] += jnp.where(lane == turn, part, 0.0)


def gathered_matrices(hidden, adapter_ids, owner_map, down_a, up_b, norm_gain, reward_head):
    rows, width = hidden.shape
    count = lax.axis_size("adapter")
    half = down_a.shape[1]
    quarter = half // 2
    rank = down_a.shape[2]
    f = lax.axis_index("fsdp")
    y = lax.axis_index("groups")
    place = jnp.stack([f, y]).astype(jnp.int32)
    order = snake(count)
    swap = [(0, 1), (1, 0)]
    params = pltpu.CompilerParams(vmem_limit_bytes=VMEM_LIMIT)

    spot = [order.index(a) for a in range(count)]
    sources = jnp.array(
        [[a] + [order[(spot[a] - d * w) % count] for d, w in ring_hops(count)] for a in range(count)],
        jnp.int32,
    )[lax.axis_index("adapter")]
    ids = jnp.repeat(sources, rank)[None, :].astype(jnp.float32)

    down_own = lax.dynamic_slice_in_dim(down_a[0].T, y * quarter, quarter, 1)
    other = lax.ppermute(
        lax.dynamic_slice_in_dim(hidden, (1 - f) * half, half, 1), "fsdp", swap
    )
    downs = ring_gather(down_own, order)

    values = hidden.astype(jnp.float32)
    factor = lax.rsqrt(jnp.mean(values * values, axis=-1, keepdims=True) + 1e-05)
    slot = owners_of(adapter_ids, owner_map)[:, None].astype(jnp.float32)
    small = jnp.concatenate([factor, slot], axis=1)
    other_small = lax.ppermute(small, "fsdp", swap)

    whole = lambda shape: pl.BlockSpec(shape, lambda i, p: (0,) * len(shape))
    bf = lambda *shape: jax.ShapeDtypeStruct(shape, jnp.bfloat16)
    fl = lambda *shape: jax.ShapeDtypeStruct(shape, jnp.float32)
    own_normed, other_normed, send = pl.pallas_call(
        norm_kernel,
        grid_spec=pltpu.PrefetchScalarGridSpec(
            num_scalar_prefetch=1,
            grid=(1,),
            in_specs=[
                pl.BlockSpec((rows, half), lambda i, p: (0, p[0])),
                whole((rows, half)),
                whole((rows, 2)),
                whole((rows, 2)),
                whole((1, half)),
            ],
            out_specs=[whole((rows, half)), whole((rows, half)), whole((rows, half + 128))],
        ),
        out_shape=[bf(rows, half), bf(rows, half), bf(rows, half + 128)],
        compiler_params=params,
        cost_estimate=pl.CostEstimate(flops=6 * rows * width, bytes_accessed=10 * rows * half, transcendentals=0),
    )(place, hidden, other, small, other_small, norm_gain[None, :])
    across = lax.ppermute(send, "groups", swap)

    here, there = pl.pallas_call(
        codes_kernel,
        grid_spec=pltpu.PrefetchScalarGridSpec(
            num_scalar_prefetch=1,
            grid=(1,),
            in_specs=[
                whole((rows, half)),
                whole((rows, half)),
                whole((rows, half + 128)),
                whole((rows, 2)),
                whole((rows, 2)),
                whole((1, count * rank)),
            ]
            + [whole((rank, quarter))] * count,
            out_specs=[whole((rows, 256)), whole((rows, 256))],
        ),
        out_shape=[fl(rows, 256), fl(rows, 256)],
        compiler_params=params,
        cost_estimate=pl.CostEstimate(flops=8 * rows * quarter * count * rank, bytes_accessed=6 * rows * half + 2 * count * rank * quarter, transcendentals=0),
    )(place, own_normed, other_normed, across, small, other_small, ids, *downs)
    here = here + lax.ppermute(there, "groups", swap)
    there = lax.ppermute(here, "fsdp", swap)

    ups = ring_gather(up_b[0], order)
    tile = 1024
    column = lambda n: pl.BlockSpec((n, tile), lambda i, p: (0, i))
    adapted, adapted_other, parts = pl.pallas_call(
        delta_kernel,
        grid_spec=pltpu.PrefetchScalarGridSpec(
            num_scalar_prefetch=1,
            grid=(half // tile,),
            in_specs=[
                column(rows),
                column(rows),
                whole((rows, 256)),
                whole((rows, 256)),
                whole((rows, 2)),
                whole((rows, 2)),
                whole((1, count * rank)),
                column(1),
            ]
            + [column(rank)] * count,
            out_specs=[
                pl.BlockSpec((rows, tile), lambda i, p: (0, p[0] * (half // tile) + i)),
                column(rows),
                whole((rows, 128)),
            ],
            scratch_shapes=[pltpu.VMEM((rows, count * rank), jnp.bfloat16)] * 2,
        ),
        out_shape=[bf(rows, width), bf(rows, half), fl(rows, 128)],
        compiler_params=params,
        cost_estimate=pl.CostEstimate(flops=4 * rows * half * count * rank, bytes_accessed=8 * rows * half + 2 * count * rank * half, transcendentals=0),
    )(place, own_normed, other_normed, here, there, small, other_small, ids, reward_head[None, :], *ups)
    adapted_back = lax.ppermute(adapted_other, "fsdp", swap)
    parts_back = lax.ppermute(parts[:, 1], "fsdp", swap)
    adapted = lax.dynamic_update_slice_in_dim(adapted, adapted_back, (1 - f) * half, 1)
    return (adapted, parts[:, 0] + parts_back)


def solution(mesh):
    placed = (
        P(("groups", "adapter", "fsdp"), None),
        P(("groups", "adapter", "fsdp"), None),
        P(),
        P("adapter", "fsdp", None),
        P("adapter", None, "fsdp"),
        P("fsdp"),
        P("fsdp"),
    )

    def per_device(*args):
        down_a, up_b = args[3], args[4]
        gathered = mesh.shape["adapter"] * 2 * (down_a.size + up_b.size)
        square = mesh.shape["groups"] == 2 and mesh.shape["fsdp"] == 2
        if square and down_a.shape[0] == 1 and down_a.shape[2] == 64 and gathered <= GATHER_LIMIT:
            return gathered_matrices(*args)
        return routed_rows(*args)

    return jax.shard_map(
        per_device,
        mesh=mesh,
        in_specs=placed,
        out_specs=(P(("groups", "adapter", "fsdp"), None), P(("groups", "adapter", "fsdp"))),
        check_vma=False,
    )
```

```python
import jax
import jax.numpy as jnp
from jax import lax
from jax.experimental import pallas as pl
from jax.experimental.pallas import tpu as pltpu
from jax.sharding import PartitionSpec as P

GATHER_LIMIT = 12 << 20
VMEM_LIMIT = 60 << 20


def routed_rows(hidden, adapter_ids, owner_map, down_a, up_b, norm_gain, reward_head):
    gain, head = (
        lax.all_gather(norm_gain, "fsdp", axis=0, tiled=True),
        lax.all_gather(reward_head, "fsdp", axis=0, tiled=True),
    )
    values = hidden.astype(jnp.float32)
    factor = lax.rsqrt(jnp.mean(values * values, axis=-1, keepdims=True) + 1e-05)
    normed = (values * factor * gain.astype(jnp.float32)).astype(jnp.bfloat16)
    row_count, width = hidden.shape
    lanes = lax.axis_size("adapter")
    capacity = max(2, (2 * row_count + lanes - 1) // lanes)
    owners = owners_of(adapter_ids, owner_map)
    marks = (owners[:, None] == jnp.arange(lanes, dtype=jnp.int32)[None, :]).astype(jnp.int32)
    ranks = jnp.sum(jnp.cumsum(marks, axis=0) * marks, axis=1) - 1
    target = owners * capacity + ranks
    outgoing = jnp.zeros((lanes * capacity, width), jnp.bfloat16).at[target].set(normed)
    outgoing = outgoing.reshape(lanes, capacity, width)
    full_a, full_b = (
        lax.all_gather(down_a, "fsdp", axis=1, tiled=True),
        lax.all_gather(up_b, "fsdp", axis=2, tiled=True),
    )
    matrix_a = full_a[0]
    matrix_b = full_b[0]
    received = lax.all_to_all(outgoing, "adapter", split_axis=0, concat_axis=0, tiled=True)
    flat = received.reshape(-1, width)
    codes = jnp.dot(flat, matrix_a, preferred_element_type=jnp.float32).astype(jnp.bfloat16)
    delta = jnp.dot(codes, matrix_b, preferred_element_type=jnp.float32).astype(jnp.bfloat16)
    returned = lax.all_to_all(
        delta.reshape(received.shape), "adapter", split_axis=0, concat_axis=0, tiled=True
    )
    delta = returned.reshape(-1, width)[target]
    adapted = (normed.astype(jnp.float32) + 2.0 * delta.astype(jnp.float32)).astype(jnp.bfloat16)
    scores = jnp.dot(adapted, head, preferred_element_type=jnp.float32)
    return (adapted, scores)


def owners_of(adapter_ids, owner_map):
    table_size = owner_map.shape[0]
    picked = (
        adapter_ids[:, 0][:, None] == jnp.arange(table_size, dtype=jnp.int32)[None, :]
    ).astype(jnp.int32)
    return jnp.sum(picked * owner_map[None, :], axis=1)


def snake(count):
    return list(range(0, count, 2)) + list(range(1, count, 2))[::-1]


def ring_hops(count):
    hops = []
    for distance in range(1, count // 2 + 1):
        hops.append((distance, 1))
        if 2 * distance < count:
            hops.append((distance, -1))
    return hops


def slots_of(lengths, first):
    left, last, order = list(lengths), [-2] * len(lengths), []
    while any(left):
        ready = [c for c in first if left[c] and last[c] <= len(order) - 2]
        ready = ready or [c for c in first if left[c]]
        chain = ready[0]
        last[chain] = len(order)
        order.append((chain, lengths[chain] - left[chain] + 1))
        left[chain] -= 1
    return order


def after(array, *others):
    return lax.optimization_barrier((array, *others))[0]


def padded(x, rows):
    return jnp.concatenate([x, jnp.zeros((rows - x.shape[0], x.shape[1]), x.dtype)], axis=0)


def norm_kernel(place, hidden, other, own_small, other_small, gain, out):
    rows, quarter = hidden.shape
    full = own_small.shape[0]
    g = gain[...].astype(jnp.float32)
    for turn, (raw, small) in enumerate(((hidden, own_small), (other, other_small))):
        normed = raw[...].astype(jnp.float32) * small[0:rows, 0:1] * g
        spot = turn * full
        out[spot : spot + full, 0:quarter] = padded(normed, full).astype(jnp.bfloat16)
        out[spot : spot + full, quarter:] = jnp.broadcast_to(small[:, 1:2], (full, 128)).astype(jnp.bfloat16)


def codes_kernel(here, across, ids, *rest):
    *downs, here_out, there_out = rest
    quarter = downs[0].shape[1]
    wide = jnp.concatenate([d[...] for d in downs], axis=0)
    names = ids[...]
    rows = jnp.concatenate([here[:, 0:quarter], across[:, 0:quarter]], axis=0)
    slot = jnp.concatenate([here[:, quarter:], across[:, quarter:]], axis=0).astype(jnp.float32)
    got = lax.dot_general(rows, wide, (((1,), (1,)), ((), ())), preferred_element_type=jnp.float32)
    total = 0.0
    for i in range(0, got.shape[1], 128):
        total = total + jnp.where(slot == names[:, i : i + 128], got[:, i : i + 128], 0.0)
    here_out[...] = total[0 : here.shape[0]]
    there_out[...] = total[here.shape[0] :]


def delta_kernel(place, mine, theirs, here, crossed, beside, beyond, own_small, other_small, ids, head, *rest):
    *ups, own_out, other_out, own_scores, other_scores, codes, sums = rest
    names = ids[...]
    full = own_small.shape[0]
    rows = own_out.shape[0]

    @pl.when(pl.program_id(0) == 0)
    def _():
        sums[...] = jnp.zeros_like(sums)
        for part, swapped, small in ((0, full, own_small), (full, 0, other_small)):
            total = here[part : part + full] + crossed[part : part + full]
            total += beside[swapped : swapped + full] + beyond[swapped : swapped + full]
            code = total + pltpu.roll(total, 64, 1)
            turned = jnp.where(place[1] == 1, pltpu.roll(code, 32, 1), code)
            lane = lax.broadcasted_iota(jnp.int32, code.shape, 1)
            first = jnp.where(lane < 64, code, turned)
            wide = jnp.concatenate([first] + [turned] * (names.shape[1] // 128 - 1), axis=1)
            wide = jnp.where(small[:, 1:2] == names, wide, 0.0)
            codes[part : part + full] = wide.astype(jnp.bfloat16)

    wide = jnp.concatenate([u[...] for u in ups], axis=0)
    weights = head[...].astype(jnp.float32)
    lane = lax.broadcasted_iota(jnp.int32, (full, 128), 1)
    deltas = jnp.dot(codes[...], wide, preferred_element_type=jnp.float32)
    is_mine = 2 * pl.program_id(0) // pl.num_programs(0) == place[1]
    for turn, out in enumerate((own_out, other_out)):
        span = slice(turn * full, (turn + 1) * full)
        normed = jnp.where(is_mine, mine[span].astype(jnp.float32), theirs[span].astype(jnp.float32))
        delta = deltas[span].astype(jnp.bfloat16).astype(jnp.float32)
        adapted = normed + 2.0 * delta
        adapted = adapted.astype(jnp.bfloat16).astype(jnp.float32)
        out[...] = adapted[0:rows].astype(jnp.bfloat16)
        part = jnp.sum(adapted * weights, axis=1, keepdims=True)
        sums[...] += jnp.where(lane == turn, part, 0.0)

    @pl.when(pl.program_id(0) == pl.num_programs(0) - 1)
    def _():
        turned = sums[...].T
        own_scores[...] = turned[0:1]
        other_scores[...] = turned[1:2]


def gathered_matrices(hidden, adapter_ids, owner_map, down_a, up_b, norm_gain, reward_head):
    rows, width = hidden.shape
    full = -(-rows // 128) * 128
    count = lax.axis_size("adapter")
    half = down_a.shape[1]
    quarter = half // 2
    rank = down_a.shape[2]
    f = lax.axis_index("fsdp")
    y = lax.axis_index("groups")
    place = jnp.stack([f, y]).astype(jnp.int32)
    order = snake(count)
    hops = ring_hops(count)
    swap = [(0, 1), (1, 0)]
    params = pltpu.CompilerParams(vmem_limit_bytes=VMEM_LIMIT)

    spot = [order.index(a) for a in range(count)]
    sources = jnp.array(
        [[a] + [order[(spot[a] - d * w) % count] for d, w in hops] for a in range(count)],
        jnp.int32,
    )[lax.axis_index("adapter")]
    ids = jnp.repeat(sources, rank)[None, :].astype(jnp.float32)
    gain, head = norm_gain[None, :], reward_head[None, :]

    cost = pl.CostEstimate(flops=1, bytes_accessed=1, transcendentals=0)
    whole = lambda shape: pl.BlockSpec(shape, lambda i, p: (0,) * len(shape))
    bf = lambda *shape: jax.ShapeDtypeStruct(shape, jnp.bfloat16)
    fl = lambda *shape: jax.ShapeDtypeStruct(shape, jnp.float32)
    tile = 1024
    each = quarter // tile
    column = lambda n: pl.BlockSpec((n, tile), lambda i, p: (0, i))
    half_column = pl.BlockSpec((rows, tile), lambda i, p: (0, p[0] * (half // tile) + i))

    perms = {
        way: [(order[i], order[(i + way) % count]) for i in range(count)] for way in (1, -1)
    }
    down_own = lax.dynamic_slice_in_dim(down_a[0].T, y * quarter, quarter, 1)
    far = count // 2
    near = far // 2
    lengths = {1: (far, count - 1 - far, near), -1: (count - 1 - far, far, near)}
    slots = {way: slots_of(lengths[way], (1, 0, 2)) for way in (1, -1)}
    held = {}
    for way in (1, -1):
        held[0, 0, way] = down_own
        for c, side in ((1, y), (2, 1 - y)):
            held[c, 0, way] = lax.dynamic_slice_in_dim(up_b[0], side * (rank // 2), rank // 2, 0)
    arrived = []

    def send_slot(k, *gates):
        now = []
        for way in (1, -1):
            if k >= len(slots[way]):
                continue
            chain, distance = slots[way][k]
            piece = held[chain, distance - 1, way]
            wait = list(gates) + (arrived[k - 2] if k >= 2 else [])
            if wait:
                piece = after(piece, *wait)
            held[chain, distance, way] = lax.ppermute(piece, "adapter", perms[way])
            now.append(held[chain, distance, way])
        arrived.append(now)

    send_slot(0)
    other = lax.ppermute(hidden, "fsdp", swap)
    values = hidden.astype(jnp.float32)
    factor = lax.rsqrt(jnp.mean(values * values, axis=-1, keepdims=True) + 1e-05)
    slot = owners_of(adapter_ids, owner_map)[:, None].astype(jnp.float32)
    small = padded(jnp.concatenate([factor, slot], axis=1), full)
    other_small = lax.ppermute(small, "fsdp", swap)
    send_slot(1)
    send_slot(2)

    def normed(gain, side):
        piece = pl.BlockSpec((rows, quarter), lambda i, p: (0, 2 * p[0] + side(p[1])))
        return pl.pallas_call(
            norm_kernel,
            grid_spec=pltpu.PrefetchScalarGridSpec(
                num_scalar_prefetch=1,
                grid=(1,),
                in_specs=[
                    piece,
                    piece,
                    whole((full, 2)),
                    whole((full, 2)),
                    pl.BlockSpec((1, quarter), lambda i, p: (0, side(p[1]))),
                ],
                out_specs=whole((2 * full, quarter + 128)),
            ),
            out_shape=bf(2 * full, quarter + 128),
            compiler_params=params,
            cost_estimate=cost,
        )(place, hidden, other, small, other_small, gain)

    theirs = normed(gain, lambda y: 1 - y)
    across = lax.ppermute(after(theirs, *arrived[1]), "groups", swap)
    gain, head, ids, *_ = lax.optimization_barrier((gain, head, ids, theirs, *arrived[2]))
    mine = normed(gain, lambda y: y)

    last_down = max(k for way in (1, -1) for k, (c, _) in enumerate(slots[way]) if c == 0)
    for k in range(3, last_down + 3):
        send_slot(k, *([mine] if k == 5 else []))
    across_far = {
        (d, w): lax.ppermute(held[1, d, w if d < far else -1], "groups", swap)
        for d, w in hops
        if near < d < far
    }
    here, there = pl.pallas_call(
        codes_kernel,
        out_shape=[fl(2 * full, 128), fl(2 * full, 128)],
        compiler_params=params,
        cost_estimate=cost,
    )(mine, across, ids, down_own, *[held[0, d, w] for d, w in hops])
    crossed = lax.ppermute(after(there, *across_far.values()), "groups", swap)
    for k in range(last_down + 3, max(len(slots[1]), len(slots[-1]))):
        send_slot(k, there)
    across_far[far, 1] = lax.ppermute(after(held[1, far, -1], there), "groups", swap)
    beside = lax.ppermute(here, "fsdp", swap)
    beyond = lax.ppermute(crossed, "fsdp", swap)

    ups = []
    for distance, way in hops:
        first = held[1, distance, way if distance < far else -1]
        ups += [first, held[2, distance, way] if distance <= near else across_far[distance, way]]
    adapted, adapted_other, own_part, other_part = pl.pallas_call(
        delta_kernel,
        grid_spec=pltpu.PrefetchScalarGridSpec(
            num_scalar_prefetch=1,
            grid=(half // tile,),
            in_specs=[
                pl.BlockSpec((2 * full, tile), lambda i, p: (0, jnp.clip(i - p[1] * each, 0, each - 1))),
                pl.BlockSpec((2 * full, tile), lambda i, p: (0, jnp.clip(i - (1 - p[1]) * each, 0, each - 1))),
            ]
            + [whole((2 * full, 128))] * 4
            + [
                whole((full, 2)),
                whole((full, 2)),
                whole((1, count * rank)),
                column(1),
                column(rank),
            ]
            + [column(rank // 2)] * len(ups),
            out_specs=[half_column, column(rows), whole((1, full)), whole((1, full))],
            scratch_shapes=[
                pltpu.VMEM((2 * full, count * rank), jnp.bfloat16),
                pltpu.VMEM((full, 128), jnp.float32),
            ],
        ),
        out_shape=[bf(rows, width), bf(rows, half), fl(1, full), fl(1, full)],
        compiler_params=params,
        cost_estimate=cost,
    )(place, mine, theirs, here, crossed, beside, beyond, small, other_small, ids, head, up_b[0], *ups)
    adapted_back = lax.ppermute(adapted_other, "fsdp", swap)
    part_back = lax.ppermute(other_part.reshape(-1), "fsdp", swap)
    adapted = lax.dynamic_update_slice_in_dim(adapted, adapted_back, (1 - f) * half, 1)
    return (adapted, (own_part.reshape(-1) + part_back)[:rows])


def solution(mesh):
    placed = (
        P(("groups", "adapter", "fsdp"), None),
        P(("groups", "adapter", "fsdp"), None),
        P(),
        P("adapter", "fsdp", None),
        P("adapter", None, "fsdp"),
        P("fsdp"),
        P("fsdp"),
    )

    def per_device(*args):
        down_a, up_b = args[3], args[4]
        gathered = mesh.shape["adapter"] * 2 * (down_a.size + up_b.size)
        square = mesh.shape["groups"] == 2 and mesh.shape["fsdp"] == 2
        if square and down_a.shape[2] == 64 and gathered <= GATHER_LIMIT:
            return gathered_matrices(*args)
        return routed_rows(*args)

    return jax.shard_map(
        per_device,
        mesh=mesh,
        in_specs=placed,
        out_specs=(P(("groups", "adapter", "fsdp"), None), P(("groups", "adapter", "fsdp"))),
        check_vma=False,
    )
```

```python
import jax
import jax.numpy as jnp
from jax import lax
from jax.experimental import pallas as pl
from jax.experimental.pallas import tpu as pltpu
from jax.sharding import PartitionSpec as P

GATHER_LIMIT = 12 << 20
VMEM_LIMIT = 32 << 20


def routed_rows(hidden, adapter_ids, owner_map, down_a, up_b, norm_gain, reward_head):
    gain, head = (
        lax.all_gather(norm_gain, "fsdp", axis=0, tiled=True),
        lax.all_gather(reward_head, "fsdp", axis=0, tiled=True),
    )
    values = hidden.astype(jnp.float32)
    factor = lax.rsqrt(jnp.mean(values * values, axis=-1, keepdims=True) + 1e-05)
    normed = (values * factor * gain.astype(jnp.float32)).astype(jnp.bfloat16)
    row_count, width = hidden.shape
    lanes = lax.axis_size("adapter")
    capacity = max(2, (2 * row_count + lanes - 1) // lanes)
    owners = owners_of(adapter_ids, owner_map)
    marks = (owners[:, None] == jnp.arange(lanes, dtype=jnp.int32)[None, :]).astype(jnp.int32)
    ranks = jnp.sum(jnp.cumsum(marks, axis=0) * marks, axis=1) - 1
    target = owners * capacity + ranks
    outgoing = jnp.zeros((lanes * capacity, width), jnp.bfloat16).at[target].set(normed)
    outgoing = outgoing.reshape(lanes, capacity, width)
    full_a, full_b = (
        lax.all_gather(down_a, "fsdp", axis=1, tiled=True),
        lax.all_gather(up_b, "fsdp", axis=2, tiled=True),
    )
    matrix_a = full_a[0]
    matrix_b = full_b[0]
    received = lax.all_to_all(outgoing, "adapter", split_axis=0, concat_axis=0, tiled=True)
    flat = received.reshape(-1, width)
    codes = jnp.dot(flat, matrix_a, preferred_element_type=jnp.float32).astype(jnp.bfloat16)
    delta = jnp.dot(codes, matrix_b, preferred_element_type=jnp.float32).astype(jnp.bfloat16)
    returned = lax.all_to_all(
        delta.reshape(received.shape), "adapter", split_axis=0, concat_axis=0, tiled=True
    )
    delta = returned.reshape(-1, width)[target]
    adapted = (normed.astype(jnp.float32) + 2.0 * delta.astype(jnp.float32)).astype(jnp.bfloat16)
    scores = jnp.dot(adapted, head, preferred_element_type=jnp.float32)
    return (adapted, scores)


def owners_of(adapter_ids, owner_map):
    table_size = owner_map.shape[0]
    picked = (
        adapter_ids[:, 0][:, None] == jnp.arange(table_size, dtype=jnp.int32)[None, :]
    ).astype(jnp.int32)
    return jnp.sum(picked * owner_map[None, :], axis=1)


def snake(count):
    return list(range(0, count, 2)) + list(range(1, count, 2))[::-1]


def ring_hops(count):
    hops = []
    for distance in range(1, count // 2 + 1):
        hops.append((distance, 1))
        if 2 * distance < count:
            hops.append((distance, -1))
    return hops


def slots_of(lengths, first):
    left, last, order = list(lengths), [-2] * len(lengths), []
    while any(left):
        ready = [c for c in first if left[c] and last[c] <= len(order) - 2]
        ready = ready or [c for c in first if left[c]]
        chain = ready[0]
        last[chain] = len(order)
        order.append((chain, lengths[chain] - left[chain] + 1))
        left[chain] -= 1
    return order


def after(array, *others):
    return lax.optimization_barrier((array, *others))[0]


def padded(x, rows):
    return jnp.concatenate([x, jnp.zeros((rows - x.shape[0], x.shape[1]), x.dtype)], axis=0)


def norm_kernel(place, hidden, other, own_small, other_small, gain, out):
    rows, quarter = hidden.shape
    full = own_small.shape[0]
    g = gain[...].astype(jnp.float32)
    for turn, (raw, small) in enumerate(((hidden, own_small), (other, other_small))):
        normed = raw[...].astype(jnp.float32) * small[0:rows, 0:1] * g
        spot = turn * full
        out[spot : spot + full, 0:quarter] = padded(normed, full).astype(jnp.bfloat16)
        out[spot : spot + full, quarter:] = jnp.broadcast_to(small[:, 1:2], (full, 128)).astype(jnp.bfloat16)


def codes_kernel(here, across, ids, *rest):
    *downs, here_out, there_out = rest
    quarter = downs[0].shape[1]
    wide = jnp.concatenate([d[...] for d in downs], axis=0)
    names = ids[...]
    rows = jnp.concatenate([here[:, 0:quarter], across[:, 0:quarter]], axis=0)
    slot = jnp.concatenate([here[:, quarter:], across[:, quarter:]], axis=0).astype(jnp.float32)
    got = lax.dot_general(rows, wide, (((1,), (1,)), ((), ())), preferred_element_type=jnp.float32)
    total = 0.0
    for i in range(0, got.shape[1], 128):
        total = total + jnp.where(slot == names[:, i : i + 128], got[:, i : i + 128], 0.0)
    here_out[...] = total[0 : here.shape[0]]
    there_out[...] = total[here.shape[0] :]


def delta_kernel(place, mine, theirs, here, crossed, beside, beyond, own_small, other_small, ids, head, *rest):
    *ups, own_out, other_out, own_scores, other_scores, codes, sums = rest
    names = ids[...]
    full = own_small.shape[0]
    rows = own_out.shape[0]

    @pl.when(pl.program_id(0) == 0)
    def _():
        sums[...] = jnp.zeros_like(sums)
        for part, swapped, small in ((0, full, own_small), (full, 0, other_small)):
            total = here[part : part + full] + crossed[part : part + full]
            total += beside[swapped : swapped + full] + beyond[swapped : swapped + full]
            code = total + pltpu.roll(total, 64, 1)
            turned = jnp.where(place[1] == 1, pltpu.roll(code, 32, 1), code)
            lane = lax.broadcasted_iota(jnp.int32, code.shape, 1)
            first = jnp.where(lane < 64, code, turned)
            wide = jnp.concatenate([first] + [turned] * (names.shape[1] // 128 - 1), axis=1)
            wide = jnp.where(small[:, 1:2] == names, wide, 0.0)
            codes[part : part + full] = wide.astype(jnp.bfloat16)

    wide = jnp.concatenate([u[...] for u in ups], axis=0)
    weights = head[...].astype(jnp.float32)
    lane = lax.broadcasted_iota(jnp.int32, (full, 128), 1)
    deltas = jnp.dot(codes[...], wide, preferred_element_type=jnp.float32)
    is_mine = 2 * pl.program_id(0) // pl.num_programs(0) == place[1]
    for turn, out in enumerate((own_out, other_out)):
        span = slice(turn * full, (turn + 1) * full)
        normed = jnp.where(is_mine, mine[span].astype(jnp.float32), theirs[span].astype(jnp.float32))
        delta = deltas[span].astype(jnp.bfloat16).astype(jnp.float32)
        adapted = normed + 2.0 * delta
        adapted = adapted.astype(jnp.bfloat16).astype(jnp.float32)
        out[...] = adapted[0:rows].astype(jnp.bfloat16)
        part = jnp.sum(adapted * weights, axis=1, keepdims=True)
        sums[...] += jnp.where(lane == turn, part, 0.0)

    @pl.when(pl.program_id(0) == pl.num_programs(0) - 1)
    def _():
        turned = sums[...].T
        own_scores[...] = turned[0:1]
        other_scores[...] = turned[1:2]


def gathered_matrices(hidden, adapter_ids, owner_map, down_a, up_b, norm_gain, reward_head):
    rows, width = hidden.shape
    full = -(-rows // 128) * 128
    count = lax.axis_size("adapter")
    half = down_a.shape[1]
    quarter = half // 2
    rank = down_a.shape[2]
    f = lax.axis_index("fsdp")
    y = lax.axis_index("groups")
    place = jnp.stack([f, y]).astype(jnp.int32)
    order = snake(count)
    hops = ring_hops(count)
    swap = [(0, 1), (1, 0)]
    params = pltpu.CompilerParams(vmem_limit_bytes=VMEM_LIMIT)

    spot = [order.index(a) for a in range(count)]
    sources = jnp.array(
        [[a] + [order[(spot[a] - d * w) % count] for d, w in hops] for a in range(count)],
        jnp.int32,
    )[lax.axis_index("adapter")]
    ids = jnp.repeat(sources, rank)[None, :].astype(jnp.float32)
    gain, head = norm_gain[None, :], reward_head[None, :]

    cost = pl.CostEstimate(flops=1, bytes_accessed=1, transcendentals=0)
    whole = lambda shape: pl.BlockSpec(shape, lambda i, p: (0,) * len(shape))
    bf = lambda *shape: jax.ShapeDtypeStruct(shape, jnp.bfloat16)
    fl = lambda *shape: jax.ShapeDtypeStruct(shape, jnp.float32)
    tile = 1024
    each = quarter // tile
    column = lambda n: pl.BlockSpec((n, tile), lambda i, p: (0, i))
    half_column = pl.BlockSpec((rows, tile), lambda i, p: (0, p[0] * (half // tile) + i))

    perms = {
        way: [(order[i], order[(i + way) % count]) for i in range(count)] for way in (1, -1)
    }
    down_own = lax.dynamic_slice_in_dim(down_a[0].T, y * quarter, quarter, 1)
    far = count // 2
    near = far // 2
    lengths = {1: (far, count - 1 - far, near), -1: (count - 1 - far, far, near)}
    slots = {way: slots_of(lengths[way], (1, 0, 2)) for way in (1, -1)}
    held = {}
    for way in (1, -1):
        held[0, 0, way] = down_own
        for c, side in ((1, y), (2, 1 - y)):
            held[c, 0, way] = lax.dynamic_slice_in_dim(up_b[0], side * (rank // 2), rank // 2, 0)
    arrived = []

    def send_slot(k, *gates):
        now = []
        for way in (1, -1):
            if k >= len(slots[way]):
                continue
            chain, distance = slots[way][k]
            piece = held[chain, distance - 1, way]
            wait = list(gates) + (arrived[k - 2] if k >= 2 else [])
            if wait:
                piece = after(piece, *wait)
            held[chain, distance, way] = lax.ppermute(piece, "adapter", perms[way])
            now.append(held[chain, distance, way])
        arrived.append(now)

    send_slot(0)
    other = lax.ppermute(hidden, "fsdp", swap)
    values = hidden.astype(jnp.float32)
    factor = lax.rsqrt(jnp.mean(values * values, axis=-1, keepdims=True) + 1e-05)
    slot = owners_of(adapter_ids, owner_map)[:, None].astype(jnp.float32)
    small = padded(jnp.concatenate([factor, slot], axis=1), full)
    other_small = lax.ppermute(small, "fsdp", swap)
    send_slot(1)
    send_slot(2)

    def normed(gain, side):
        piece = pl.BlockSpec((rows, quarter), lambda i, p: (0, 2 * p[0] + side(p[1])))
        return pl.pallas_call(
            norm_kernel,
            grid_spec=pltpu.PrefetchScalarGridSpec(
                num_scalar_prefetch=1,
                grid=(1,),
                in_specs=[
                    piece,
                    piece,
                    whole((full, 2)),
                    whole((full, 2)),
                    pl.BlockSpec((1, quarter), lambda i, p: (0, side(p[1]))),
                ],
                out_specs=whole((2 * full, quarter + 128)),
            ),
            out_shape=bf(2 * full, quarter + 128),
            compiler_params=params,
            cost_estimate=cost,
        )(place, hidden, other, small, other_small, gain)

    theirs = normed(gain, lambda y: 1 - y)
    across = lax.ppermute(after(theirs, *arrived[1]), "groups", swap)
    gain, head, ids, *_ = lax.optimization_barrier((gain, head, ids, theirs, *arrived[2]))
    mine = normed(gain, lambda y: y)

    last_down = max(k for way in (1, -1) for k, (c, _) in enumerate(slots[way]) if c == 0)
    for k in range(3, last_down + 3):
        send_slot(k, *([mine] if k == 5 else []))
    across_far = {
        (d, w): lax.ppermute(held[1, d, w if d < far else -1], "groups", swap)
        for d, w in hops
        if near < d < far
    }
    here, there = pl.pallas_call(
        codes_kernel,
        out_shape=[fl(2 * full, 128), fl(2 * full, 128)],
        compiler_params=params,
        cost_estimate=cost,
    )(mine, across, ids, down_own, *[held[0, d, w] for d, w in hops])
    crossed = lax.ppermute(after(there, *across_far.values()), "groups", swap)
    for k in range(last_down + 3, max(len(slots[1]), len(slots[-1]))):
        send_slot(k, there)
    across_far[far, 1] = lax.ppermute(after(held[1, far, -1], there), "groups", swap)
    beside = lax.ppermute(here, "fsdp", swap)
    beyond = lax.ppermute(crossed, "fsdp", swap)

    ups = []
    for distance, way in hops:
        first = held[1, distance, way if distance < far else -1]
        ups += [first, held[2, distance, way] if distance <= near else across_far[distance, way]]
    adapted, adapted_other, own_part, other_part = pl.pallas_call(
        delta_kernel,
        grid_spec=pltpu.PrefetchScalarGridSpec(
            num_scalar_prefetch=1,
            grid=(half // tile,),
            in_specs=[
                pl.BlockSpec((2 * full, tile), lambda i, p: (0, jnp.clip(i - p[1] * each, 0, each - 1))),
                pl.BlockSpec((2 * full, tile), lambda i, p: (0, jnp.clip(i - (1 - p[1]) * each, 0, each - 1))),
            ]
            + [whole((2 * full, 128))] * 4
            + [
                whole((full, 2)),
                whole((full, 2)),
                whole((1, count * rank)),
                column(1),
                column(rank),
            ]
            + [column(rank // 2)] * len(ups),
            out_specs=[half_column, column(rows), whole((1, full)), whole((1, full))],
            scratch_shapes=[
                pltpu.VMEM((2 * full, count * rank), jnp.bfloat16),
                pltpu.VMEM((full, 128), jnp.float32),
            ],
        ),
        out_shape=[bf(rows, width), bf(rows, half), fl(1, full), fl(1, full)],
        compiler_params=params,
        cost_estimate=cost,
    )(place, mine, theirs, here, crossed, beside, beyond, small, other_small, ids, head, up_b[0], *ups)
    adapted_back = lax.ppermute(adapted_other, "fsdp", swap)
    part_back = lax.ppermute(other_part.reshape(-1), "fsdp", swap)
    adapted = lax.dynamic_update_slice_in_dim(adapted, adapted_back, (1 - f) * half, 1)
    return (adapted, (own_part.reshape(-1) + part_back)[:rows])


def solution(mesh):
    placed = (
        P(("groups", "adapter", "fsdp"), None),
        P(("groups", "adapter", "fsdp"), None),
        P(),
        P("adapter", "fsdp", None),
        P("adapter", None, "fsdp"),
        P("fsdp"),
        P("fsdp"),
    )

    def per_device(*args):
        down_a, up_b = args[3], args[4]
        gathered = mesh.shape["adapter"] * 2 * (down_a.size + up_b.size)
        square = mesh.shape["groups"] == 2 and mesh.shape["fsdp"] == 2
        if square and down_a.shape[2] == 64 and gathered <= GATHER_LIMIT:
            return gathered_matrices(*args)
        return routed_rows(*args)

    return jax.shard_map(
        per_device,
        mesh=mesh,
        in_specs=placed,
        out_specs=(P(("groups", "adapter", "fsdp"), None), P(("groups", "adapter", "fsdp"))),
        check_vma=False,
    )
```

```python
import jax
import jax.numpy as jnp
from jax import lax
from jax.experimental import pallas as pl
from jax.experimental.pallas import tpu as pltpu
from jax.sharding import PartitionSpec as P

GATHER_LIMIT = 12 << 20
VMEM_LIMIT = 32 << 20


def routed_rows(hidden, adapter_ids, owner_map, down_a, up_b, norm_gain, reward_head):
    gain, head = (
        lax.all_gather(norm_gain, "fsdp", axis=0, tiled=True),
        lax.all_gather(reward_head, "fsdp", axis=0, tiled=True),
    )
    values = hidden.astype(jnp.float32)
    factor = lax.rsqrt(jnp.mean(values * values, axis=-1, keepdims=True) + 1e-05)
    normed = (values * factor * gain.astype(jnp.float32)).astype(jnp.bfloat16)
    row_count, width = hidden.shape
    lanes = lax.axis_size("adapter")
    capacity = max(2, (2 * row_count + lanes - 1) // lanes)
    owners = owners_of(adapter_ids, owner_map)
    marks = (owners[:, None] == jnp.arange(lanes, dtype=jnp.int32)[None, :]).astype(jnp.int32)
    ranks = jnp.sum(jnp.cumsum(marks, axis=0) * marks, axis=1) - 1
    target = owners * capacity + ranks
    outgoing = jnp.zeros((lanes * capacity, width), jnp.bfloat16).at[target].set(normed)
    outgoing = outgoing.reshape(lanes, capacity, width)
    full_a, full_b = (
        lax.all_gather(down_a, "fsdp", axis=1, tiled=True),
        lax.all_gather(up_b, "fsdp", axis=2, tiled=True),
    )
    matrix_a = full_a[0]
    matrix_b = full_b[0]
    received = lax.all_to_all(outgoing, "adapter", split_axis=0, concat_axis=0, tiled=True)
    flat = received.reshape(-1, width)
    codes = jnp.dot(flat, matrix_a, preferred_element_type=jnp.float32).astype(jnp.bfloat16)
    delta = jnp.dot(codes, matrix_b, preferred_element_type=jnp.float32).astype(jnp.bfloat16)
    returned = lax.all_to_all(
        delta.reshape(received.shape), "adapter", split_axis=0, concat_axis=0, tiled=True
    )
    delta = returned.reshape(-1, width)[target]
    adapted = (normed.astype(jnp.float32) + 2.0 * delta.astype(jnp.float32)).astype(jnp.bfloat16)
    scores = jnp.dot(adapted, head, preferred_element_type=jnp.float32)
    return (adapted, scores)


def owners_of(adapter_ids, owner_map):
    table_size = owner_map.shape[0]
    picked = (
        adapter_ids[:, 0][:, None] == jnp.arange(table_size, dtype=jnp.int32)[None, :]
    ).astype(jnp.int32)
    return jnp.sum(picked * owner_map[None, :], axis=1)


def snake(count):
    return list(range(0, count, 2)) + list(range(1, count, 2))[::-1]


def ring_hops(count):
    hops = []
    for distance in range(1, count // 2 + 1):
        hops.append((distance, 1))
        if 2 * distance < count:
            hops.append((distance, -1))
    return hops


def slots_of(lengths, first):
    left, last, order = list(lengths), [-2] * len(lengths), []
    while any(left):
        ready = [c for c in first if left[c] and last[c] <= len(order) - 2]
        ready = ready or [c for c in first if left[c]]
        chain = ready[0]
        last[chain] = len(order)
        order.append((chain, lengths[chain] - left[chain] + 1))
        left[chain] -= 1
    return order


def after(array, *others):
    return lax.optimization_barrier((array, *others))[0]


def padded(x, rows):
    return jnp.concatenate([x, jnp.zeros((rows - x.shape[0], x.shape[1]), x.dtype)], axis=0)


def norm_kernel(place, hidden, other, own_small, other_small, gain, out):
    rows, quarter = hidden.shape
    full = own_small.shape[0]
    g = gain[...].astype(jnp.float32)
    for turn, (raw, small) in enumerate(((hidden, own_small), (other, other_small))):
        normed = raw[...].astype(jnp.float32) * small[0:rows, 0:1] * g
        spot = turn * full
        out[spot : spot + full, 0:quarter] = padded(normed, full).astype(jnp.bfloat16)
        out[spot : spot + full, quarter:] = jnp.broadcast_to(small[:, 1:2], (full, 128)).astype(jnp.bfloat16)


def codes_kernel(here, across, ids, *rest):
    *downs, here_out, there_out = rest
    quarter = downs[0].shape[1]
    wide = jnp.concatenate([d[...] for d in downs], axis=0)
    names = ids[...]
    rows = jnp.concatenate([here[:, 0:quarter], across[:, 0:quarter]], axis=0)
    slot = jnp.concatenate([here[:, quarter:], across[:, quarter:]], axis=0).astype(jnp.float32)
    got = lax.dot_general(rows, wide, (((1,), (1,)), ((), ())), preferred_element_type=jnp.float32)
    total = 0.0
    for i in range(0, got.shape[1], 128):
        total = total + jnp.where(slot == names[:, i : i + 128], got[:, i : i + 128], 0.0)
    here_out[...] = total[0 : here.shape[0]]
    there_out[...] = total[here.shape[0] :]


def delta_kernel(place, mine, theirs, here, crossed, beside, beyond, own_small, other_small, ids, head, *rest):
    *ups, own_out, other_out, own_scores, other_scores, codes, sums = rest
    names = ids[...]
    full = own_small.shape[0]
    rows = own_out.shape[0]

    @pl.when(pl.program_id(0) == 0)
    def _():
        sums[...] = jnp.zeros_like(sums)
        for part, swapped, small in ((0, full, own_small), (full, 0, other_small)):
            total = here[part : part + full] + crossed[part : part + full]
            total += beside[swapped : swapped + full] + beyond[swapped : swapped + full]
            code = total + pltpu.roll(total, 64, 1)
            turned = jnp.where(place[1] == 1, pltpu.roll(code, 32, 1), code)
            lane = lax.broadcasted_iota(jnp.int32, code.shape, 1)
            first = jnp.where(lane < 64, code, turned)
            wide = jnp.concatenate([first] + [turned] * (names.shape[1] // 128 - 1), axis=1)
            wide = jnp.where(small[:, 1:2] == names, wide, 0.0)
            codes[part : part + full] = wide.astype(jnp.bfloat16)

    wide = jnp.concatenate([u[...] for u in ups], axis=0)
    weights = head[...].astype(jnp.float32)
    lane = lax.broadcasted_iota(jnp.int32, (full, 128), 1)
    deltas = jnp.dot(codes[...], wide, preferred_element_type=jnp.float32)
    is_mine = 2 * pl.program_id(0) // pl.num_programs(0) == place[1]
    for turn, out in enumerate((own_out, other_out)):
        span = slice(turn * full, (turn + 1) * full)
        normed = jnp.where(is_mine, mine[span].astype(jnp.float32), theirs[span].astype(jnp.float32))
        delta = deltas[span].astype(jnp.bfloat16).astype(jnp.float32)
        adapted = normed + 2.0 * delta
        adapted = adapted.astype(jnp.bfloat16).astype(jnp.float32)
        out[...] = adapted[0:rows].astype(jnp.bfloat16)
        part = jnp.sum(adapted * weights, axis=1, keepdims=True)
        sums[...] += jnp.where(lane == turn, part, 0.0)

    @pl.when(pl.program_id(0) == pl.num_programs(0) - 1)
    def _():
        turned = sums[...].T
        own_scores[...] = turned[0:1]
        other_scores[...] = turned[1:2]


def gathered_matrices(hidden, adapter_ids, owner_map, down_a, up_b, norm_gain, reward_head):
    rows, width = hidden.shape
    full = -(-rows // 128) * 128
    count = lax.axis_size("adapter")
    half = down_a.shape[1]
    quarter = half // 2
    rank = down_a.shape[2]
    f = lax.axis_index("fsdp")
    y = lax.axis_index("groups")
    place = jnp.stack([f, y]).astype(jnp.int32)
    order = snake(count)
    hops = ring_hops(count)
    swap = [(0, 1), (1, 0)]
    params = pltpu.CompilerParams(vmem_limit_bytes=VMEM_LIMIT)

    spot = [order.index(a) for a in range(count)]
    sources = jnp.array(
        [[a] + [order[(spot[a] - d * w) % count] for d, w in hops] for a in range(count)],
        jnp.int32,
    )[lax.axis_index("adapter")]
    ids = jnp.repeat(sources, rank)[None, :].astype(jnp.float32)
    gain, head = norm_gain[None, :], reward_head[None, :]

    cost = pl.CostEstimate(flops=1, bytes_accessed=1, transcendentals=0)
    whole = lambda shape: pl.BlockSpec(shape, lambda i, p: (0,) * len(shape))
    bf = lambda *shape: jax.ShapeDtypeStruct(shape, jnp.bfloat16)
    fl = lambda *shape: jax.ShapeDtypeStruct(shape, jnp.float32)
    tile = 2048
    each = quarter // tile
    column = lambda n: pl.BlockSpec((n, tile), lambda i, p: (0, i))
    half_column = pl.BlockSpec((rows, tile), lambda i, p: (0, p[0] * (half // tile) + i))

    perms = {
        way: [(order[i], order[(i + way) % count]) for i in range(count)] for way in (1, -1)
    }
    down_own = lax.dynamic_slice_in_dim(down_a[0].T, y * quarter, quarter, 1)
    far = count // 2
    near = far // 2
    lengths = {1: (far, count - 1 - far, near), -1: (count - 1 - far, far, near)}
    slots = {way: slots_of(lengths[way], (1, 0, 2)) for way in (1, -1)}
    held = {}
    for way in (1, -1):
        held[0, 0, way] = down_own
        for c, side in ((1, y), (2, 1 - y)):
            held[c, 0, way] = lax.dynamic_slice_in_dim(up_b[0], side * (rank // 2), rank // 2, 0)
    arrived = []

    def send_slot(k, *gates):
        now = []
        for way in (1, -1):
            if k >= len(slots[way]):
                continue
            chain, distance = slots[way][k]
            piece = held[chain, distance - 1, way]
            wait = list(gates) + (arrived[k - 2] if k >= 2 else [])
            if wait:
                piece = after(piece, *wait)
            held[chain, distance, way] = lax.ppermute(piece, "adapter", perms[way])
            now.append(held[chain, distance, way])
        arrived.append(now)

    send_slot(0)
    other = lax.ppermute(hidden, "fsdp", swap)
    values = hidden.astype(jnp.float32)
    factor = lax.rsqrt(jnp.mean(values * values, axis=-1, keepdims=True) + 1e-05)
    slot = owners_of(adapter_ids, owner_map)[:, None].astype(jnp.float32)
    small = padded(jnp.concatenate([factor, slot], axis=1), full)
    other_small = lax.ppermute(small, "fsdp", swap)
    send_slot(1)
    send_slot(2)

    def normed(gain, side):
        piece = pl.BlockSpec((rows, quarter), lambda i, p: (0, 2 * p[0] + side(p[1])))
        return pl.pallas_call(
            norm_kernel,
            grid_spec=pltpu.PrefetchScalarGridSpec(
                num_scalar_prefetch=1,
                grid=(1,),
                in_specs=[
                    piece,
                    piece,
                    whole((full, 2)),
                    whole((full, 2)),
                    pl.BlockSpec((1, quarter), lambda i, p: (0, side(p[1]))),
                ],
                out_specs=whole((2 * full, quarter + 128)),
            ),
            out_shape=bf(2 * full, quarter + 128),
            compiler_params=params,
            cost_estimate=cost,
        )(place, hidden, other, small, other_small, gain)

    theirs = normed(gain, lambda y: 1 - y)
    across = lax.ppermute(after(theirs, *arrived[1]), "groups", swap)
    gain, head, ids, *_ = lax.optimization_barrier((gain, head, ids, theirs, *arrived[2]))
    mine = normed(gain, lambda y: y)

    last_down = max(k for way in (1, -1) for k, (c, _) in enumerate(slots[way]) if c == 0)
    across_far = {}
    for k in range(3, last_down + 1):
        send_slot(k, *([mine] if k == 5 else []))
    for d, w in hops:
        if near < d < far:
            across_far[d, w] = lax.ppermute(held[1, d, w], "groups", swap)
    for k in range(last_down + 1, max(len(slots[1]), len(slots[-1]))):
        send_slot(k, *across_far.values())
    here, there = pl.pallas_call(
        codes_kernel,
        out_shape=[fl(2 * full, 128), fl(2 * full, 128)],
        compiler_params=params,
        cost_estimate=cost,
    )(mine, across, ids, down_own, *[held[0, d, w] for d, w in hops])
    across_far[far, 1] = lax.ppermute(held[1, far, -1], "groups", swap)
    crossed = lax.ppermute(after(there, across_far[far, 1]), "groups", swap)
    beside = lax.ppermute(here, "fsdp", swap)
    beyond = lax.ppermute(crossed, "fsdp", swap)

    ups = []
    for distance, way in hops:
        first = held[1, distance, way if distance < far else -1]
        ups += [first, held[2, distance, way] if distance <= near else across_far[distance, way]]
    adapted, adapted_other, own_part, other_part = pl.pallas_call(
        delta_kernel,
        grid_spec=pltpu.PrefetchScalarGridSpec(
            num_scalar_prefetch=1,
            grid=(half // tile,),
            in_specs=[
                pl.BlockSpec((2 * full, tile), lambda i, p: (0, jnp.clip(i - p[1] * each, 0, each - 1))),
                pl.BlockSpec((2 * full, tile), lambda i, p: (0, jnp.clip(i - (1 - p[1]) * each, 0, each - 1))),
            ]
            + [whole((2 * full, 128))] * 4
            + [
                whole((full, 2)),
                whole((full, 2)),
                whole((1, count * rank)),
                column(1),
                column(rank),
            ]
            + [column(rank // 2)] * len(ups),
            out_specs=[half_column, column(rows), whole((1, full)), whole((1, full))],
            scratch_shapes=[
                pltpu.VMEM((2 * full, count * rank), jnp.bfloat16),
                pltpu.VMEM((full, 128), jnp.float32),
            ],
        ),
        out_shape=[bf(rows, width), bf(rows, half), fl(1, full), fl(1, full)],
        compiler_params=params,
        cost_estimate=cost,
    )(place, mine, theirs, here, crossed, beside, beyond, small, other_small, ids, head, up_b[0], *ups)
    adapted_back = lax.ppermute(adapted_other, "fsdp", swap)
    part_back = lax.ppermute(other_part.reshape(-1), "fsdp", swap)
    adapted = lax.dynamic_update_slice_in_dim(adapted, adapted_back, (1 - f) * half, 1)
    return (adapted, (own_part.reshape(-1) + part_back)[:rows])


def solution(mesh):
    placed = (
        P(("groups", "adapter", "fsdp"), None),
        P(("groups", "adapter", "fsdp"), None),
        P(),
        P("adapter", "fsdp", None),
        P("adapter", None, "fsdp"),
        P("fsdp"),
        P("fsdp"),
    )

    def per_device(*args):
        down_a, up_b = args[3], args[4]
        gathered = mesh.shape["adapter"] * 2 * (down_a.size + up_b.size)
        square = mesh.shape["groups"] == 2 and mesh.shape["fsdp"] == 2
        if square and down_a.shape[2] == 64 and gathered <= GATHER_LIMIT:
            return gathered_matrices(*args)
        return routed_rows(*args)

    return jax.shard_map(
        per_device,
        mesh=mesh,
        in_specs=placed,
        out_specs=(P(("groups", "adapter", "fsdp"), None), P(("groups", "adapter", "fsdp"))),
        check_vma=False,
    )
```

```python
import jax
import jax.numpy as jnp
from jax import lax
from jax.experimental import pallas as pl
from jax.experimental.pallas import tpu as pltpu
from jax.sharding import PartitionSpec as P

GATHER_LIMIT = 12 << 20
VMEM_LIMIT = 32 << 20


def routed_rows(hidden, adapter_ids, owner_map, down_a, up_b, norm_gain, reward_head):
    gain, head = (
        lax.all_gather(norm_gain, "fsdp", axis=0, tiled=True),
        lax.all_gather(reward_head, "fsdp", axis=0, tiled=True),
    )
    values = hidden.astype(jnp.float32)
    factor = lax.rsqrt(jnp.mean(values * values, axis=-1, keepdims=True) + 1e-05)
    normed = (values * factor * gain.astype(jnp.float32)).astype(jnp.bfloat16)
    row_count, width = hidden.shape
    lanes = lax.axis_size("adapter")
    capacity = max(2, (2 * row_count + lanes - 1) // lanes)
    owners = owners_of(adapter_ids, owner_map)
    marks = (owners[:, None] == jnp.arange(lanes, dtype=jnp.int32)[None, :]).astype(jnp.int32)
    ranks = jnp.sum(jnp.cumsum(marks, axis=0) * marks, axis=1) - 1
    target = owners * capacity + ranks
    outgoing = jnp.zeros((lanes * capacity, width), jnp.bfloat16).at[target].set(normed)
    outgoing = outgoing.reshape(lanes, capacity, width)
    full_a, full_b = (
        lax.all_gather(down_a, "fsdp", axis=1, tiled=True),
        lax.all_gather(up_b, "fsdp", axis=2, tiled=True),
    )
    matrix_a = full_a[0]
    matrix_b = full_b[0]
    received = lax.all_to_all(outgoing, "adapter", split_axis=0, concat_axis=0, tiled=True)
    flat = received.reshape(-1, width)
    codes = jnp.dot(flat, matrix_a, preferred_element_type=jnp.float32).astype(jnp.bfloat16)
    delta = jnp.dot(codes, matrix_b, preferred_element_type=jnp.float32).astype(jnp.bfloat16)
    returned = lax.all_to_all(
        delta.reshape(received.shape), "adapter", split_axis=0, concat_axis=0, tiled=True
    )
    delta = returned.reshape(-1, width)[target]
    adapted = (normed.astype(jnp.float32) + 2.0 * delta.astype(jnp.float32)).astype(jnp.bfloat16)
    scores = jnp.dot(adapted, head, preferred_element_type=jnp.float32)
    return (adapted, scores)


def owners_of(adapter_ids, owner_map):
    table_size = owner_map.shape[0]
    picked = (
        adapter_ids[:, 0][:, None] == jnp.arange(table_size, dtype=jnp.int32)[None, :]
    ).astype(jnp.int32)
    return jnp.sum(picked * owner_map[None, :], axis=1)


def snake(count):
    return list(range(0, count, 2)) + list(range(1, count, 2))[::-1]


def ring_hops(count):
    hops = []
    for distance in range(1, count // 2 + 1):
        hops.append((distance, 1))
        if 2 * distance < count:
            hops.append((distance, -1))
    return hops


def slots_of(lengths, first):
    left, last, order = list(lengths), [-2] * len(lengths), []
    while any(left):
        ready = [c for c in first if left[c] and last[c] <= len(order) - 2]
        ready = ready or [c for c in first if left[c]]
        chain = ready[0]
        last[chain] = len(order)
        order.append((chain, lengths[chain] - left[chain] + 1))
        left[chain] -= 1
    return order


def after(array, *others):
    return lax.optimization_barrier((array, *others))[0]


def padded(x, rows):
    return jnp.concatenate([x, jnp.zeros((rows - x.shape[0], x.shape[1]), x.dtype)], axis=0)


def norm_kernel(place, hidden, other, own_small, other_small, gain, out):
    rows, quarter = hidden.shape
    full = own_small.shape[0]
    g = gain[...].astype(jnp.float32)
    for turn, (raw, small) in enumerate(((hidden, own_small), (other, other_small))):
        normed = raw[...].astype(jnp.float32) * small[0:rows, 0:1] * g
        spot = turn * full
        out[spot : spot + full, 0:quarter] = padded(normed, full).astype(jnp.bfloat16)
        out[spot : spot + full, quarter:] = jnp.broadcast_to(small[:, 1:2], (full, 128)).astype(jnp.bfloat16)


def codes_kernel(here, across, ids, *rest):
    *downs, here_out, there_out = rest
    quarter = downs[0].shape[1]
    wide = jnp.concatenate([d[...] for d in downs], axis=0)
    names = ids[...]
    rows = jnp.concatenate([here[:, 0:quarter], across[:, 0:quarter]], axis=0)
    slot = jnp.concatenate([here[:, quarter:], across[:, quarter:]], axis=0).astype(jnp.float32)
    got = lax.dot_general(rows, wide, (((1,), (1,)), ((), ())), preferred_element_type=jnp.float32)
    total = 0.0
    for i in range(0, got.shape[1], 128):
        total = total + jnp.where(slot == names[:, i : i + 128], got[:, i : i + 128], 0.0)
    here_out[...] = total[0 : here.shape[0]]
    there_out[...] = total[here.shape[0] :]


def delta_kernel(place, mine, theirs, here, crossed, beside, beyond, own_small, other_small, ids, head, *rest):
    *ups, own_out, other_out, own_scores, other_scores, codes, sums = rest
    names = ids[...]
    full = own_small.shape[0]
    rows = own_out.shape[0]

    @pl.when(pl.program_id(0) == 0)
    def _():
        sums[...] = jnp.zeros_like(sums)
        for part, swapped, small in ((0, full, own_small), (full, 0, other_small)):
            total = here[part : part + full] + crossed[part : part + full]
            total += beside[swapped : swapped + full] + beyond[swapped : swapped + full]
            code = total + pltpu.roll(total, 64, 1)
            turned = jnp.where(place[1] == 1, pltpu.roll(code, 32, 1), code)
            lane = lax.broadcasted_iota(jnp.int32, code.shape, 1)
            first = jnp.where(lane < 64, code, turned)
            wide = jnp.concatenate([first] + [turned] * (names.shape[1] // 128 - 1), axis=1)
            wide = jnp.where(small[:, 1:2] == names, wide, 0.0)
            codes[part : part + full] = wide.astype(jnp.bfloat16)

    wide = jnp.concatenate([u[...] for u in ups], axis=0)
    weights = head[...].astype(jnp.float32)
    lane = lax.broadcasted_iota(jnp.int32, (full, 128), 1)
    deltas = jnp.dot(codes[...], wide, preferred_element_type=jnp.float32)
    is_mine = 2 * pl.program_id(0) // pl.num_programs(0) == place[1]
    for turn, out in enumerate((own_out, other_out)):
        span = slice(turn * full, (turn + 1) * full)
        normed = jnp.where(is_mine, mine[span].astype(jnp.float32), theirs[span].astype(jnp.float32))
        delta = deltas[span].astype(jnp.bfloat16).astype(jnp.float32)
        adapted = normed + 2.0 * delta
        adapted = adapted.astype(jnp.bfloat16).astype(jnp.float32)
        out[...] = adapted[0:rows].astype(jnp.bfloat16)
        part = jnp.sum(adapted * weights, axis=1, keepdims=True)
        sums[...] += jnp.where(lane == turn, part, 0.0)

    @pl.when(pl.program_id(0) == pl.num_programs(0) - 1)
    def _():
        turned = sums[...].T
        own_scores[...] = turned[0:1]
        other_scores[...] = turned[1:2]


def gathered_matrices(hidden, adapter_ids, owner_map, down_a, up_b, norm_gain, reward_head):
    rows, width = hidden.shape
    full = -(-rows // 128) * 128
    count = lax.axis_size("adapter")
    half = down_a.shape[1]
    quarter = half // 2
    rank = down_a.shape[2]
    f = lax.axis_index("fsdp")
    y = lax.axis_index("groups")
    place = jnp.stack([f, y]).astype(jnp.int32)
    order = snake(count)
    hops = ring_hops(count)
    swap = [(0, 1), (1, 0)]
    params = pltpu.CompilerParams(vmem_limit_bytes=VMEM_LIMIT)

    spot = [order.index(a) for a in range(count)]
    sources = jnp.array(
        [[a] + [order[(spot[a] - d * w) % count] for d, w in hops] for a in range(count)],
        jnp.int32,
    )[lax.axis_index("adapter")]
    ids = jnp.repeat(sources, rank)[None, :].astype(jnp.float32)
    gain, head = norm_gain[None, :], reward_head[None, :]

    cost = pl.CostEstimate(flops=1, bytes_accessed=1, transcendentals=0)
    whole = lambda shape: pl.BlockSpec(shape, lambda i, p: (0,) * len(shape))
    bf = lambda *shape: jax.ShapeDtypeStruct(shape, jnp.bfloat16)
    fl = lambda *shape: jax.ShapeDtypeStruct(shape, jnp.float32)
    tile = 2048
    each = quarter // tile
    column = lambda n: pl.BlockSpec((n, tile), lambda i, p: (0, i))
    half_column = pl.BlockSpec((rows, tile), lambda i, p: (0, p[0] * (half // tile) + i))

    perms = {
        way: [(order[i], order[(i + way) % count]) for i in range(count)] for way in (1, -1)
    }
    down_own = lax.dynamic_slice_in_dim(down_a[0].T, y * quarter, quarter, 1)
    far = count // 2
    near = far // 2
    lengths = {1: (far, count - 1 - far, near), -1: (count - 1 - far, far, near)}
    slots = {way: slots_of(lengths[way], (1, 0, 2)) for way in (1, -1)}
    if count == 8:
        for way, chains in ((1, (1, 0, 2, 1, 0, 1, 0, 0, 2)), (-1, (1, 0, 2, 1, 0, 1, 0, 1, 2))):
            left = {c: iter(range(1, n + 1)) for c, n in enumerate(lengths[way])}
            slots[way] = [(c, next(left[c])) for c in chains]
    held = {}
    for way in (1, -1):
        held[0, 0, way] = down_own
        for c, side in ((1, y), (2, 1 - y)):
            held[c, 0, way] = lax.dynamic_slice_in_dim(up_b[0], side * (rank // 2), rank // 2, 0)
    arrived = []

    def send_slot(k, *gates):
        now = []
        for way in (1, -1):
            if k >= len(slots[way]):
                continue
            chain, distance = slots[way][k]
            piece = held[chain, distance - 1, way]
            wait = list(gates) + (arrived[k - 2] if k >= 3 else [])
            if wait:
                piece = after(piece, *wait)
            held[chain, distance, way] = lax.ppermute(piece, "adapter", perms[way])
            now.append(held[chain, distance, way])
        arrived.append(now)

    send_slot(0)
    other = lax.ppermute(hidden, "fsdp", swap)
    values = hidden.astype(jnp.float32)
    factor = lax.rsqrt(jnp.mean(values * values, axis=-1, keepdims=True) + 1e-05)
    slot = owners_of(adapter_ids, owner_map)[:, None].astype(jnp.float32)
    small = padded(jnp.concatenate([factor, slot], axis=1), full)
    other_small = lax.ppermute(small, "fsdp", swap)
    send_slot(1)
    send_slot(2)

    def normed(gain, side):
        piece = pl.BlockSpec((rows, quarter), lambda i, p: (0, 2 * p[0] + side(p[1])))
        return pl.pallas_call(
            norm_kernel,
            grid_spec=pltpu.PrefetchScalarGridSpec(
                num_scalar_prefetch=1,
                grid=(1,),
                in_specs=[
                    piece,
                    piece,
                    whole((full, 2)),
                    whole((full, 2)),
                    pl.BlockSpec((1, quarter), lambda i, p: (0, side(p[1]))),
                ],
                out_specs=whole((2 * full, quarter + 128)),
            ),
            out_shape=bf(2 * full, quarter + 128),
            compiler_params=params,
            cost_estimate=cost,
        )(place, hidden, other, small, other_small, gain)

    theirs = normed(gain, lambda y: 1 - y)
    across = lax.ppermute(after(theirs, *arrived[1]), "groups", swap)
    gain, head, ids, *_ = lax.optimization_barrier((gain, head, ids, theirs, *arrived[2]))
    mine = normed(gain, lambda y: y)

    last_down = max(k for way in (1, -1) for k, (c, _) in enumerate(slots[way]) if c == 0)
    across_far = {}
    for k in range(3, last_down + 1):
        send_slot(k, *([mine] if k == 5 else []))
    for d, w in hops:
        if near < d < far:
            across_far[d, w] = lax.ppermute(held[1, d, w], "groups", swap)
    for k in range(last_down + 1, max(len(slots[1]), len(slots[-1]))):
        send_slot(k, across_far[far - 1, 1])
    here, there = pl.pallas_call(
        codes_kernel,
        out_shape=[fl(2 * full, 128), fl(2 * full, 128)],
        compiler_params=params,
        cost_estimate=cost,
    )(mine, across, ids, down_own, *[held[0, d, w] for d, w in hops])
    across_far[far, 1] = lax.ppermute(held[1, far, -1], "groups", swap)
    crossed = lax.ppermute(after(there, across_far[far, 1]), "groups", swap)
    beside = lax.ppermute(here, "fsdp", swap)
    beyond = lax.ppermute(crossed, "fsdp", swap)

    ups = []
    for distance, way in hops:
        first = held[1, distance, way if distance < far else -1]
        ups += [first, held[2, distance, way] if distance <= near else across_far[distance, way]]
    adapted, adapted_other, own_part, other_part = pl.pallas_call(
        delta_kernel,
        grid_spec=pltpu.PrefetchScalarGridSpec(
            num_scalar_prefetch=1,
            grid=(half // tile,),
            in_specs=[
                pl.BlockSpec((2 * full, tile), lambda i, p: (0, jnp.clip(i - p[1] * each, 0, each - 1))),
                pl.BlockSpec((2 * full, tile), lambda i, p: (0, jnp.clip(i - (1 - p[1]) * each, 0, each - 1))),
            ]
            + [whole((2 * full, 128))] * 4
            + [
                whole((full, 2)),
                whole((full, 2)),
                whole((1, count * rank)),
                column(1),
                column(rank),
            ]
            + [column(rank // 2)] * len(ups),
            out_specs=[half_column, column(rows), whole((1, full)), whole((1, full))],
            scratch_shapes=[
                pltpu.VMEM((2 * full, count * rank), jnp.bfloat16),
                pltpu.VMEM((full, 128), jnp.float32),
            ],
        ),
        out_shape=[bf(rows, width), bf(rows, half), fl(1, full), fl(1, full)],
        compiler_params=params,
        cost_estimate=cost,
    )(place, mine, theirs, here, crossed, beside, beyond, small, other_small, ids, head, up_b[0], *ups)
    adapted_back = lax.ppermute(adapted_other, "fsdp", swap)
    part_back = lax.ppermute(other_part.reshape(-1), "fsdp", swap)
    adapted = lax.dynamic_update_slice_in_dim(adapted, adapted_back, (1 - f) * half, 1)
    return (adapted, (own_part.reshape(-1) + part_back)[:rows])


def solution(mesh):
    placed = (
        P(("groups", "adapter", "fsdp"), None),
        P(("groups", "adapter", "fsdp"), None),
        P(),
        P("adapter", "fsdp", None),
        P("adapter", None, "fsdp"),
        P("fsdp"),
        P("fsdp"),
    )

    def per_device(*args):
        down_a, up_b = args[3], args[4]
        gathered = mesh.shape["adapter"] * 2 * (down_a.size + up_b.size)
        square = mesh.shape["groups"] == 2 and mesh.shape["fsdp"] == 2
        if square and down_a.shape[2] == 64 and gathered <= GATHER_LIMIT:
            return gathered_matrices(*args)
        return routed_rows(*args)

    return jax.shard_map(
        per_device,
        mesh=mesh,
        in_specs=placed,
        out_specs=(P(("groups", "adapter", "fsdp"), None), P(("groups", "adapter", "fsdp"))),
        check_vma=False,
    )
```

```python
import jax
import jax.numpy as jnp
from jax import lax
from jax.experimental import pallas as pl
from jax.experimental.pallas import tpu as pltpu
from jax.sharding import PartitionSpec as P

GATHER_LIMIT = 12 << 20
VMEM_LIMIT = 32 << 20


def routed_rows(hidden, adapter_ids, owner_map, down_a, up_b, norm_gain, reward_head):
    gain, head = (
        lax.all_gather(norm_gain, "fsdp", axis=0, tiled=True),
        lax.all_gather(reward_head, "fsdp", axis=0, tiled=True),
    )
    values = hidden.astype(jnp.float32)
    factor = lax.rsqrt(jnp.mean(values * values, axis=-1, keepdims=True) + 1e-05)
    normed = (values * factor * gain.astype(jnp.float32)).astype(jnp.bfloat16)
    row_count, width = hidden.shape
    lanes = lax.axis_size("adapter")
    capacity = max(2, (2 * row_count + lanes - 1) // lanes)
    owners = owners_of(adapter_ids, owner_map)
    marks = (owners[:, None] == jnp.arange(lanes, dtype=jnp.int32)[None, :]).astype(jnp.int32)
    ranks = jnp.sum(jnp.cumsum(marks, axis=0) * marks, axis=1) - 1
    target = owners * capacity + ranks
    outgoing = jnp.zeros((lanes * capacity, width), jnp.bfloat16).at[target].set(normed)
    outgoing = outgoing.reshape(lanes, capacity, width)
    full_a, full_b = (
        lax.all_gather(down_a, "fsdp", axis=1, tiled=True),
        lax.all_gather(up_b, "fsdp", axis=2, tiled=True),
    )
    matrix_a = full_a[0]
    matrix_b = full_b[0]
    received = lax.all_to_all(outgoing, "adapter", split_axis=0, concat_axis=0, tiled=True)
    flat = received.reshape(-1, width)
    codes = jnp.dot(flat, matrix_a, preferred_element_type=jnp.float32).astype(jnp.bfloat16)
    delta = jnp.dot(codes, matrix_b, preferred_element_type=jnp.float32).astype(jnp.bfloat16)
    returned = lax.all_to_all(
        delta.reshape(received.shape), "adapter", split_axis=0, concat_axis=0, tiled=True
    )
    delta = returned.reshape(-1, width)[target]
    adapted = (normed.astype(jnp.float32) + 2.0 * delta.astype(jnp.float32)).astype(jnp.bfloat16)
    scores = jnp.dot(adapted, head, preferred_element_type=jnp.float32)
    return (adapted, scores)


def owners_of(adapter_ids, owner_map):
    table_size = owner_map.shape[0]
    picked = (
        adapter_ids[:, 0][:, None] == jnp.arange(table_size, dtype=jnp.int32)[None, :]
    ).astype(jnp.int32)
    return jnp.sum(picked * owner_map[None, :], axis=1)


def snake(count):
    return list(range(0, count, 2)) + list(range(1, count, 2))[::-1]


def ring_hops(count):
    hops = []
    for distance in range(1, count // 2 + 1):
        hops.append((distance, 1))
        if 2 * distance < count:
            hops.append((distance, -1))
    return hops


def slots_of(lengths, first):
    left, last, order = list(lengths), [-2] * len(lengths), []
    while any(left):
        ready = [c for c in first if left[c] and last[c] <= len(order) - 2]
        ready = ready or [c for c in first if left[c]]
        chain = ready[0]
        last[chain] = len(order)
        order.append((chain, lengths[chain] - left[chain] + 1))
        left[chain] -= 1
    return order


def after(array, *others):
    return lax.optimization_barrier((array, *others))[0]


def padded(x, rows):
    return jnp.concatenate([x, jnp.zeros((rows - x.shape[0], x.shape[1]), x.dtype)], axis=0)


def norm_kernel(place, hidden, other, own_small, other_small, gain, out):
    rows, quarter = hidden.shape
    full = own_small.shape[0]
    g = gain[...].astype(jnp.float32)
    for turn, (raw, small) in enumerate(((hidden, own_small), (other, other_small))):
        normed = raw[...].astype(jnp.float32) * small[0:rows, 0:1] * g
        spot = turn * full
        out[spot : spot + full, 0:quarter] = padded(normed, full).astype(jnp.bfloat16)
        out[spot : spot + full, quarter:] = jnp.broadcast_to(small[:, 1:2], (full, 128)).astype(jnp.bfloat16)


def codes_kernel(here, across, ids, *rest):
    *downs, here_out, there_out = rest
    quarter = downs[0].shape[1]
    wide = jnp.concatenate([d[...] for d in downs], axis=0)
    names = ids[...]
    rows = jnp.concatenate([here[:, 0:quarter], across[:, 0:quarter]], axis=0)
    slot = jnp.concatenate([here[:, quarter:], across[:, quarter:]], axis=0).astype(jnp.float32)
    got = lax.dot_general(rows, wide, (((1,), (1,)), ((), ())), preferred_element_type=jnp.float32)
    total = 0.0
    for i in range(0, got.shape[1], 128):
        total = total + jnp.where(slot == names[:, i : i + 128], got[:, i : i + 128], 0.0)
    here_out[...] = total[0 : here.shape[0]]
    there_out[...] = total[here.shape[0] :]


def delta_kernel(place, mine, theirs, here, crossed, beside, beyond, own_small, other_small, ids, head, *rest):
    *ups, own_out, other_out, own_scores, other_scores, codes, sums = rest
    names = ids[...]
    full = own_small.shape[0]
    rows = own_out.shape[0]

    @pl.when(pl.program_id(0) == 0)
    def _():
        sums[...] = jnp.zeros_like(sums)
        for part, swapped, small in ((0, full, own_small), (full, 0, other_small)):
            total = here[part : part + full] + crossed[part : part + full]
            total += beside[swapped : swapped + full] + beyond[swapped : swapped + full]
            code = total + pltpu.roll(total, 64, 1)
            turned = jnp.where(place[1] == 1, pltpu.roll(code, 32, 1), code)
            lane = lax.broadcasted_iota(jnp.int32, code.shape, 1)
            first = jnp.where(lane < 64, code, turned)
            wide = jnp.concatenate([first] + [turned] * (names.shape[1] // 128 - 1), axis=1)
            wide = jnp.where(small[:, 1:2] == names, wide, 0.0)
            codes[part : part + full] = wide.astype(jnp.bfloat16)

    wide = jnp.concatenate([u[...] for u in ups], axis=0)
    weights = head[...].astype(jnp.float32)
    lane = lax.broadcasted_iota(jnp.int32, (full, 128), 1)
    deltas = jnp.dot(codes[...], wide, preferred_element_type=jnp.float32)
    is_mine = 2 * pl.program_id(0) // pl.num_programs(0) == place[1]
    for turn, out in enumerate((own_out, other_out)):
        span = slice(turn * full, (turn + 1) * full)
        normed = jnp.where(is_mine, mine[span].astype(jnp.float32), theirs[span].astype(jnp.float32))
        delta = deltas[span].astype(jnp.bfloat16).astype(jnp.float32)
        adapted = normed + 2.0 * delta
        adapted = adapted.astype(jnp.bfloat16).astype(jnp.float32)
        out[...] = adapted[0:rows].astype(jnp.bfloat16)
        part = jnp.sum(adapted * weights, axis=1, keepdims=True)
        sums[...] += jnp.where(lane == turn, part, 0.0)

    @pl.when(pl.program_id(0) == pl.num_programs(0) - 1)
    def _():
        turned = sums[...].T
        own_scores[...] = turned[0:1]
        other_scores[...] = turned[1:2]


def gathered_matrices(hidden, adapter_ids, owner_map, down_a, up_b, norm_gain, reward_head):
    rows, width = hidden.shape
    full = -(-rows // 128) * 128
    count = lax.axis_size("adapter")
    half = down_a.shape[1]
    quarter = half // 2
    rank = down_a.shape[2]
    f = lax.axis_index("fsdp")
    y = lax.axis_index("groups")
    place = jnp.stack([f, y]).astype(jnp.int32)
    order = snake(count)
    hops = ring_hops(count)
    swap = [(0, 1), (1, 0)]
    params = pltpu.CompilerParams(vmem_limit_bytes=VMEM_LIMIT)

    spot = [order.index(a) for a in range(count)]
    sources = jnp.array(
        [[a] + [order[(spot[a] - d * w) % count] for d, w in hops] for a in range(count)],
        jnp.int32,
    )[lax.axis_index("adapter")]
    ids = jnp.repeat(sources, rank)[None, :].astype(jnp.float32)
    gain, head = norm_gain[None, :], reward_head[None, :]

    cost = pl.CostEstimate(flops=1, bytes_accessed=1, transcendentals=0)
    whole = lambda shape: pl.BlockSpec(shape, lambda i, p: (0,) * len(shape))
    bf = lambda *shape: jax.ShapeDtypeStruct(shape, jnp.bfloat16)
    fl = lambda *shape: jax.ShapeDtypeStruct(shape, jnp.float32)
    tile = 2048
    each = quarter // tile
    column = lambda n: pl.BlockSpec((n, tile), lambda i, p: (0, i))
    half_column = pl.BlockSpec((rows, tile), lambda i, p: (0, p[0] * (half // tile) + i))

    perms = {
        way: [(order[i], order[(i + way) % count]) for i in range(count)] for way in (1, -1)
    }
    down_own = lax.dynamic_slice_in_dim(down_a[0].T, y * quarter, quarter, 1)
    far = count // 2
    near = far // 2
    lengths = {1: (far, count - 1 - far, near), -1: (count - 1 - far, far, near)}
    slots = {way: slots_of(lengths[way], (1, 0, 2)) for way in (1, -1)}
    if count == 8:
        for way, chains in ((1, (1, 0, 2, 1, 0, 1, 0, 0, 2)), (-1, (1, 0, 2, 1, 0, 1, 0, 1, 2))):
            left = {c: iter(range(1, n + 1)) for c, n in enumerate(lengths[way])}
            slots[way] = [(c, next(left[c])) for c in chains]
    held = {}
    for way in (1, -1):
        held[0, 0, way] = down_own
        for c, side in ((1, y), (2, 1 - y)):
            held[c, 0, way] = lax.dynamic_slice_in_dim(up_b[0], side * (rank // 2), rank // 2, 0)
    arrived = []

    def send_slot(k, *gates):
        now = []
        for way in (1, -1):
            if k >= len(slots[way]):
                continue
            chain, distance = slots[way][k]
            piece = held[chain, distance - 1, way]
            wait = list(gates) + (arrived[k - 2] if k >= 3 else [])
            if wait:
                piece = after(piece, *wait)
            held[chain, distance, way] = lax.ppermute(piece, "adapter", perms[way])
            now.append(held[chain, distance, way])
        arrived.append(now)

    send_slot(0)
    other = lax.ppermute(hidden, "fsdp", swap)
    values = hidden.astype(jnp.float32)
    factor = lax.rsqrt(jnp.mean(values * values, axis=-1, keepdims=True) + 1e-05)
    slot = owners_of(adapter_ids, owner_map)[:, None].astype(jnp.float32)
    small = padded(jnp.concatenate([factor, slot], axis=1), full)
    other_small = lax.ppermute(small, "fsdp", swap)
    send_slot(1)
    send_slot(2)

    def normed(gain, side):
        piece = pl.BlockSpec((rows, quarter), lambda i, p: (0, 2 * p[0] + side(p[1])))
        return pl.pallas_call(
            norm_kernel,
            grid_spec=pltpu.PrefetchScalarGridSpec(
                num_scalar_prefetch=1,
                grid=(1,),
                in_specs=[
                    piece,
                    piece,
                    whole((full, 2)),
                    whole((full, 2)),
                    pl.BlockSpec((1, quarter), lambda i, p: (0, side(p[1]))),
                ],
                out_specs=whole((2 * full, quarter + 128)),
            ),
            out_shape=bf(2 * full, quarter + 128),
            compiler_params=params,
            cost_estimate=cost,
        )(place, hidden, other, small, other_small, gain)

    theirs = normed(gain, lambda y: 1 - y)
    across = lax.ppermute(after(theirs, *arrived[1]), "groups", swap)
    gain, head, ids, *_ = lax.optimization_barrier((gain, head, ids, theirs, *arrived[2]))
    mine = normed(gain, lambda y: y)

    last_down = max(k for way in (1, -1) for k, (c, _) in enumerate(slots[way]) if c == 0)
    across_far = {}
    for k in range(3, last_down + 1):
        send_slot(k, *([mine] if k == 6 else []))
    for d, w in hops:
        if near < d < far:
            across_far[d, w] = lax.ppermute(held[1, d, w], "groups", swap)
    for k in range(last_down + 1, max(len(slots[1]), len(slots[-1]))):
        send_slot(k, across_far[far - 1, 1])
    here, there = pl.pallas_call(
        codes_kernel,
        out_shape=[fl(2 * full, 128), fl(2 * full, 128)],
        compiler_params=params,
        cost_estimate=cost,
    )(mine, across, ids, down_own, *[held[0, d, w] for d, w in hops])
    across_far[far, 1] = lax.ppermute(held[1, far, -1], "groups", swap)
    crossed = lax.ppermute(after(there, across_far[far, 1]), "groups", swap)
    beside = lax.ppermute(here, "fsdp", swap)
    beyond = lax.ppermute(crossed, "fsdp", swap)

    ups = []
    for distance, way in hops:
        first = held[1, distance, way if distance < far else -1]
        ups += [first, held[2, distance, way] if distance <= near else across_far[distance, way]]
    adapted, adapted_other, own_part, other_part = pl.pallas_call(
        delta_kernel,
        grid_spec=pltpu.PrefetchScalarGridSpec(
            num_scalar_prefetch=1,
            grid=(half // tile,),
            in_specs=[
                pl.BlockSpec((2 * full, tile), lambda i, p: (0, jnp.clip(i - p[1] * each, 0, each - 1))),
                pl.BlockSpec((2 * full, tile), lambda i, p: (0, jnp.clip(i - (1 - p[1]) * each, 0, each - 1))),
            ]
            + [whole((2 * full, 128))] * 4
            + [
                whole((full, 2)),
                whole((full, 2)),
                whole((1, count * rank)),
                column(1),
                column(rank),
            ]
            + [column(rank // 2)] * len(ups),
            out_specs=[half_column, column(rows), whole((1, full)), whole((1, full))],
            scratch_shapes=[
                pltpu.VMEM((2 * full, count * rank), jnp.bfloat16),
                pltpu.VMEM((full, 128), jnp.float32),
            ],
        ),
        out_shape=[bf(rows, width), bf(rows, half), fl(1, full), fl(1, full)],
        compiler_params=params,
        cost_estimate=cost,
    )(place, mine, theirs, here, crossed, beside, beyond, small, other_small, ids, head, up_b[0], *ups)
    adapted_back = lax.ppermute(adapted_other, "fsdp", swap)
    part_back = lax.ppermute(other_part.reshape(-1), "fsdp", swap)
    adapted = lax.dynamic_update_slice_in_dim(adapted, adapted_back, (1 - f) * half, 1)
    return (adapted, (own_part.reshape(-1) + part_back)[:rows])


def solution(mesh):
    placed = (
        P(("groups", "adapter", "fsdp"), None),
        P(("groups", "adapter", "fsdp"), None),
        P(),
        P("adapter", "fsdp", None),
        P("adapter", None, "fsdp"),
        P("fsdp"),
        P("fsdp"),
    )

    def per_device(*args):
        down_a, up_b = args[3], args[4]
        gathered = mesh.shape["adapter"] * 2 * (down_a.size + up_b.size)
        square = mesh.shape["groups"] == 2 and mesh.shape["fsdp"] == 2
        if square and down_a.shape[2] == 64 and gathered <= GATHER_LIMIT:
            return gathered_matrices(*args)
        return routed_rows(*args)

    return jax.shard_map(
        per_device,
        mesh=mesh,
        in_specs=placed,
        out_specs=(P(("groups", "adapter", "fsdp"), None), P(("groups", "adapter", "fsdp"))),
        check_vma=False,
    )
```

```python
import jax
import jax.numpy as jnp
from jax import lax
from jax.experimental import pallas as pl
from jax.experimental.pallas import tpu as pltpu
from jax.sharding import PartitionSpec as P

GATHER_LIMIT = 12 << 20
VMEM_LIMIT = 32 << 20


def routed_rows(hidden, adapter_ids, owner_map, down_a, up_b, norm_gain, reward_head):
    gain, head = (
        lax.all_gather(norm_gain, "fsdp", axis=0, tiled=True),
        lax.all_gather(reward_head, "fsdp", axis=0, tiled=True),
    )
    values = hidden.astype(jnp.float32)
    factor = lax.rsqrt(jnp.mean(values * values, axis=-1, keepdims=True) + 1e-05)
    normed = (values * factor * gain.astype(jnp.float32)).astype(jnp.bfloat16)
    row_count, width = hidden.shape
    lanes = lax.axis_size("adapter")
    capacity = max(2, (2 * row_count + lanes - 1) // lanes)
    owners = owners_of(adapter_ids, owner_map)
    marks = (owners[:, None] == jnp.arange(lanes, dtype=jnp.int32)[None, :]).astype(jnp.int32)
    ranks = jnp.sum(jnp.cumsum(marks, axis=0) * marks, axis=1) - 1
    target = owners * capacity + ranks
    outgoing = jnp.zeros((lanes * capacity, width), jnp.bfloat16).at[target].set(normed)
    outgoing = outgoing.reshape(lanes, capacity, width)
    full_a, full_b = (
        lax.all_gather(down_a, "fsdp", axis=1, tiled=True),
        lax.all_gather(up_b, "fsdp", axis=2, tiled=True),
    )
    matrix_a = full_a[0]
    matrix_b = full_b[0]
    received = lax.all_to_all(outgoing, "adapter", split_axis=0, concat_axis=0, tiled=True)
    flat = received.reshape(-1, width)
    codes = jnp.dot(flat, matrix_a, preferred_element_type=jnp.float32).astype(jnp.bfloat16)
    delta = jnp.dot(codes, matrix_b, preferred_element_type=jnp.float32).astype(jnp.bfloat16)
    returned = lax.all_to_all(
        delta.reshape(received.shape), "adapter", split_axis=0, concat_axis=0, tiled=True
    )
    delta = returned.reshape(-1, width)[target]
    adapted = (normed.astype(jnp.float32) + 2.0 * delta.astype(jnp.float32)).astype(jnp.bfloat16)
    scores = jnp.dot(adapted, head, preferred_element_type=jnp.float32)
    return (adapted, scores)


def owners_of(adapter_ids, owner_map):
    table_size = owner_map.shape[0]
    picked = (
        adapter_ids[:, 0][:, None] == jnp.arange(table_size, dtype=jnp.int32)[None, :]
    ).astype(jnp.int32)
    return jnp.sum(picked * owner_map[None, :], axis=1)


def snake(count):
    return list(range(0, count, 2)) + list(range(1, count, 2))[::-1]


def ring_hops(count):
    hops = []
    for distance in range(1, count // 2 + 1):
        hops.append((distance, 1))
        if 2 * distance < count:
            hops.append((distance, -1))
    return hops


def slots_of(lengths, first):
    left, last, order = list(lengths), [-2] * len(lengths), []
    while any(left):
        ready = [c for c in first if left[c] and last[c] <= len(order) - 2]
        ready = ready or [c for c in first if left[c]]
        chain = ready[0]
        last[chain] = len(order)
        order.append((chain, lengths[chain] - left[chain] + 1))
        left[chain] -= 1
    return order


def after(array, *others):
    return lax.optimization_barrier((array, *others))[0]


def padded(x, rows):
    return jnp.concatenate([x, jnp.zeros((rows - x.shape[0], x.shape[1]), x.dtype)], axis=0)


def norm_kernel(place, hidden, other, own_small, other_small, gain, out):
    rows, quarter = hidden.shape
    full = own_small.shape[0]
    g = gain[...].astype(jnp.float32)
    for turn, (raw, small) in enumerate(((hidden, own_small), (other, other_small))):
        normed = raw[...].astype(jnp.float32) * small[0:rows, 0:1] * g
        spot = turn * full
        out[spot : spot + full, 0:quarter] = padded(normed, full).astype(jnp.bfloat16)
        out[spot : spot + full, quarter:] = jnp.broadcast_to(small[:, 1:2], (full, 128)).astype(jnp.bfloat16)


def codes_kernel(here, across, ids, *rest):
    *downs, here_out, there_out = rest
    quarter = downs[0].shape[1]
    wide = jnp.concatenate([d[...] for d in downs], axis=0)
    names = ids[...]
    rows = jnp.concatenate([here[:, 0:quarter], across[:, 0:quarter]], axis=0)
    slot = jnp.concatenate([here[:, quarter:], across[:, quarter:]], axis=0).astype(jnp.float32)
    got = lax.dot_general(rows, wide, (((1,), (1,)), ((), ())), preferred_element_type=jnp.float32)
    total = 0.0
    for i in range(0, got.shape[1], 128):
        total = total + jnp.where(slot == names[:, i : i + 128], got[:, i : i + 128], 0.0)
    here_out[...] = total[0 : here.shape[0]]
    there_out[...] = total[here.shape[0] :]


def delta_kernel(place, mine, theirs, here, crossed, beside, beyond, own_small, other_small, ids, head, *rest):
    *ups, own_out, other_out, own_scores, other_scores, codes, sums = rest
    names = ids[...]
    full = own_small.shape[0]
    rows = own_out.shape[0]

    @pl.when(pl.program_id(0) == 0)
    def _():
        sums[...] = jnp.zeros_like(sums)
        for part, swapped, small in ((0, full, own_small), (full, 0, other_small)):
            total = here[part : part + full] + crossed[part : part + full]
            total += beside[swapped : swapped + full] + beyond[swapped : swapped + full]
            code = total + pltpu.roll(total, 64, 1)
            turned = jnp.where(place[1] == 1, pltpu.roll(code, 32, 1), code)
            lane = lax.broadcasted_iota(jnp.int32, code.shape, 1)
            first = jnp.where(lane < 64, code, turned)
            wide = jnp.concatenate([first] + [turned] * (names.shape[1] // 128 - 1), axis=1)
            wide = jnp.where(small[:, 1:2] == names, wide, 0.0)
            codes[part : part + full] = wide.astype(jnp.bfloat16)

    wide = jnp.concatenate([u[...] for u in ups], axis=0)
    weights = head[...].astype(jnp.float32)
    lane = lax.broadcasted_iota(jnp.int32, (full, 128), 1)
    deltas = jnp.dot(codes[...], wide, preferred_element_type=jnp.float32)
    is_mine = 2 * pl.program_id(0) // pl.num_programs(0) == place[1]
    for turn, out in enumerate((own_out, other_out)):
        span = slice(turn * full, (turn + 1) * full)
        normed = jnp.where(is_mine, mine[span].astype(jnp.float32), theirs[span].astype(jnp.float32))
        delta = deltas[span].astype(jnp.bfloat16).astype(jnp.float32)
        adapted = normed + 2.0 * delta
        adapted = adapted.astype(jnp.bfloat16).astype(jnp.float32)
        out[...] = adapted[0:rows].astype(jnp.bfloat16)
        part = jnp.sum(adapted * weights, axis=1, keepdims=True)
        sums[...] += jnp.where(lane == turn, part, 0.0)

    @pl.when(pl.program_id(0) == pl.num_programs(0) - 1)
    def _():
        turned = sums[...].T
        own_scores[...] = turned[0:1]
        other_scores[...] = turned[1:2]


def gathered_matrices(hidden, adapter_ids, owner_map, down_a, up_b, norm_gain, reward_head):
    rows, width = hidden.shape
    full = -(-rows // 128) * 128
    count = lax.axis_size("adapter")
    half = down_a.shape[1]
    quarter = half // 2
    rank = down_a.shape[2]
    f = lax.axis_index("fsdp")
    y = lax.axis_index("groups")
    place = jnp.stack([f, y]).astype(jnp.int32)
    order = snake(count)
    hops = ring_hops(count)
    swap = [(0, 1), (1, 0)]
    params = pltpu.CompilerParams(vmem_limit_bytes=VMEM_LIMIT)

    spot = [order.index(a) for a in range(count)]
    sources = jnp.array(
        [[a] + [order[(spot[a] - d * w) % count] for d, w in hops] for a in range(count)],
        jnp.int32,
    )[lax.axis_index("adapter")]
    ids = jnp.repeat(sources, rank)[None, :].astype(jnp.float32)
    gain, head = norm_gain[None, :], reward_head[None, :]

    cost = pl.CostEstimate(flops=1, bytes_accessed=1, transcendentals=0)
    whole = lambda shape: pl.BlockSpec(shape, lambda i, p: (0,) * len(shape))
    bf = lambda *shape: jax.ShapeDtypeStruct(shape, jnp.bfloat16)
    fl = lambda *shape: jax.ShapeDtypeStruct(shape, jnp.float32)
    tile = 2048
    each = quarter // tile
    column = lambda n: pl.BlockSpec((n, tile), lambda i, p: (0, i))
    half_column = pl.BlockSpec((rows, tile), lambda i, p: (0, p[0] * (half // tile) + i))

    perms = {
        way: [(order[i], order[(i + way) % count]) for i in range(count)] for way in (1, -1)
    }
    down_own = lax.dynamic_slice_in_dim(down_a[0].T, y * quarter, quarter, 1)
    far = count // 2
    near = far // 2
    lengths = {1: (far, count - 1 - far, near), -1: (count - 1 - far, far, near)}
    slots = {way: slots_of(lengths[way], (1, 0, 2)) for way in (1, -1)}
    if count == 8:
        for way, chains in ((1, (1, 0, 2, 1, 0, 1, 0, 0, 2)), (-1, (1, 0, 2, 1, 0, 1, 0, 1, 2))):
            left = {c: iter(range(1, n + 1)) for c, n in enumerate(lengths[way])}
            slots[way] = [(c, next(left[c])) for c in chains]
    held = {}
    for way in (1, -1):
        held[0, 0, way] = down_own
        for c, side in ((1, y), (2, 1 - y)):
            held[c, 0, way] = lax.dynamic_slice_in_dim(up_b[0], side * (rank // 2), rank // 2, 0)
    arrived = []

    def send_slot(k, *gates):
        now = []
        for way in (1, -1):
            if k >= len(slots[way]):
                continue
            chain, distance = slots[way][k]
            piece = held[chain, distance - 1, way]
            wait = list(gates) + (arrived[k - 2] if k >= 3 else [])
            if wait:
                piece = after(piece, *wait)
            held[chain, distance, way] = lax.ppermute(piece, "adapter", perms[way])
            now.append(held[chain, distance, way])
        arrived.append(now)

    send_slot(0)
    other = lax.ppermute(hidden, "fsdp", swap)
    values = hidden.astype(jnp.float32)
    factor = lax.rsqrt(jnp.mean(values * values, axis=-1, keepdims=True) + 1e-05)
    slot = owners_of(adapter_ids, owner_map)[:, None].astype(jnp.float32)
    small = padded(jnp.concatenate([factor, slot], axis=1), full)
    other_small = lax.ppermute(small, "fsdp", swap)
    send_slot(1)
    send_slot(2)

    def normed(gain, side):
        piece = pl.BlockSpec((rows, quarter), lambda i, p: (0, 2 * p[0] + side(p[1])))
        return pl.pallas_call(
            norm_kernel,
            grid_spec=pltpu.PrefetchScalarGridSpec(
                num_scalar_prefetch=1,
                grid=(1,),
                in_specs=[
                    piece,
                    piece,
                    whole((full, 2)),
                    whole((full, 2)),
                    pl.BlockSpec((1, quarter), lambda i, p: (0, side(p[1]))),
                ],
                out_specs=whole((2 * full, quarter + 128)),
            ),
            out_shape=bf(2 * full, quarter + 128),
            compiler_params=params,
            cost_estimate=cost,
        )(place, hidden, other, small, other_small, gain)

    theirs = normed(gain, lambda y: 1 - y)
    across = lax.ppermute(after(theirs, *arrived[1]), "groups", swap)
    gain, head, ids, *_ = lax.optimization_barrier((gain, head, ids, theirs, *arrived[1]))
    mine = normed(gain, lambda y: y)

    last_down = max(k for way in (1, -1) for k, (c, _) in enumerate(slots[way]) if c == 0)
    across_far = {}
    for k in range(3, last_down + 1):
        send_slot(k, *([mine] if k == 6 else []))
    for d, w in hops:
        if near < d < far:
            across_far[d, w] = lax.ppermute(held[1, d, w], "groups", swap)
    for k in range(last_down + 1, max(len(slots[1]), len(slots[-1]))):
        send_slot(k, across_far[far - 1, 1])
    here, there = pl.pallas_call(
        codes_kernel,
        out_shape=[fl(2 * full, 128), fl(2 * full, 128)],
        compiler_params=params,
        cost_estimate=cost,
    )(mine, across, ids, down_own, *[held[0, d, w] for d, w in hops])
    across_far[far, 1] = lax.ppermute(held[1, far, -1], "groups", swap)
    crossed = lax.ppermute(after(there, across_far[far, 1]), "groups", swap)
    beside = lax.ppermute(here, "fsdp", swap)
    beyond = lax.ppermute(crossed, "fsdp", swap)

    ups = []
    for distance, way in hops:
        first = held[1, distance, way if distance < far else -1]
        ups += [first, held[2, distance, way] if distance <= near else across_far[distance, way]]
    adapted, adapted_other, own_part, other_part = pl.pallas_call(
        delta_kernel,
        grid_spec=pltpu.PrefetchScalarGridSpec(
            num_scalar_prefetch=1,
            grid=(half // tile,),
            in_specs=[
                pl.BlockSpec((2 * full, tile), lambda i, p: (0, jnp.clip(i - p[1] * each, 0, each - 1))),
                pl.BlockSpec((2 * full, tile), lambda i, p: (0, jnp.clip(i - (1 - p[1]) * each, 0, each - 1))),
            ]
            + [whole((2 * full, 128))] * 4
            + [
                whole((full, 2)),
                whole((full, 2)),
                whole((1, count * rank)),
                column(1),
                column(rank),
            ]
            + [column(rank // 2)] * len(ups),
            out_specs=[half_column, column(rows), whole((1, full)), whole((1, full))],
            scratch_shapes=[
                pltpu.VMEM((2 * full, count * rank), jnp.bfloat16),
                pltpu.VMEM((full, 128), jnp.float32),
            ],
        ),
        out_shape=[bf(rows, width), bf(rows, half), fl(1, full), fl(1, full)],
        compiler_params=params,
        cost_estimate=cost,
    )(place, mine, theirs, here, crossed, beside, beyond, small, other_small, ids, head, up_b[0], *ups)
    adapted_back = lax.ppermute(adapted_other, "fsdp", swap)
    part_back = lax.ppermute(other_part.reshape(-1), "fsdp", swap)
    adapted = lax.dynamic_update_slice_in_dim(adapted, adapted_back, (1 - f) * half, 1)
    return (adapted, (own_part.reshape(-1) + part_back)[:rows])


def solution(mesh):
    placed = (
        P(("groups", "adapter", "fsdp"), None),
        P(("groups", "adapter", "fsdp"), None),
        P(),
        P("adapter", "fsdp", None),
        P("adapter", None, "fsdp"),
        P("fsdp"),
        P("fsdp"),
    )

    def per_device(*args):
        down_a, up_b = args[3], args[4]
        gathered = mesh.shape["adapter"] * 2 * (down_a.size + up_b.size)
        square = mesh.shape["groups"] == 2 and mesh.shape["fsdp"] == 2
        if square and down_a.shape[2] == 64 and gathered <= GATHER_LIMIT:
            return gathered_matrices(*args)
        return routed_rows(*args)

    return jax.shard_map(
        per_device,
        mesh=mesh,
        in_specs=placed,
        out_specs=(P(("groups", "adapter", "fsdp"), None), P(("groups", "adapter", "fsdp"))),
        check_vma=False,
    )
```
